512 devices in a mesh: grp: 8 (over x_lo, y), slab: 64 (over z, x_hi, core).
Axes of the slice: x: 4 (x_hi: 2, x_lo: 2; x = x_hi * 2 + x_lo), y: 4, z: 16, core: 2. Of those that a mesh axis runs over, the one named last changes fastest.
Arguments:
- velocity: float32 [64, 512, 512], P('grp', 'slab'), may hold values from -6 to 6
- rate: float32 [64, 512, 512], P('grp', 'slab'), may hold values from 0.02 to 0.16
- forcing: float32 [64, 512, 512], P('grp', 'slab'), may hold values from -3 to 3
- anchor_line: int32 [8192], P(('grp', 'slab')), may hold values from 0 to 63
- anchor_z: int32 [8192], P(('grp', 'slab')), may hold values from 0 to 384
- assign: int32 [8192, 1], P(('grp', 'slab')), may hold values from 0 to 63; in each aligned block of 16 rows (0 to 15, 16 to 31, ...) at most 2 rows name the same one
- spectral: float32 [2048, 64], replicated, may hold values from -0.75 to 0.75
- dense: float32 [68, 64], replicated, may hold values from -4 to 4
- momentum: float32 [2048, 64], P(('grp', 'slab')), may hold values from -0.3125 to 0.3125
Outputs:
- field_out: float32 [64, 512, 512], P('grp', 'slab')
- trainer_loss: float32 [8, 64], P('grp', 'slab')
- spectral_new: float32 [2048, 64], replicated
- dense_new: float32 [68, 64], replicated
- momentum_new: float32 [2048, 64], P(('grp', 'slab'))
The draws below stay inside these ranges and needn't reach their ends.
Inputs may be any that keep to these rules, and one draw needn't show every extreme that they name: `assign`: within the 16 lines of one device no trainer is named more than 2 times, and in some device's lines one trainer is named exactly 2 times.
All inputs are finite; a program needn't handle non-finite values.
Results may differ from the reference program's by a relative error of at most 0.0001.
Values sent between devices are 32-bit elements; how exact they have to be, the bound alone decides.
A program may use at most 64 MiB of HBM per device.

```python
import math
import jax
import jax.numpy as jnp
import numpy as np
from jax import lax

CX = 8
CY = 8
CZ = 512
ROWS = 16
STEPS = 2
SUB = 128
MODES = 16
WIDTH = 64
CAP = 2
NX = 64
NY = 512
TOTAL = 8192
N_GRP = 8
N_SLAB = 64


def place_ends(drawn, rng, low, largest):
    index_at = [jax.random.randint(jax.random.fold_in(rng, axis), (), 0, length) for axis, length in enumerate(drawn.shape)]
    longest = drawn.shape.index(max(drawn.shape))
    beside = index_at[:longest] + [(index_at[longest] + 1) % drawn.shape[longest]] + index_at[longest + 1:]
    return drawn.at[tuple(index_at)].set(low).at[tuple(beside)].set(largest)


def block_levels(rng, dims, shards, smallest, top_value):
    def one(position, blocks):
        steps = jax.random.uniform(jax.random.fold_in(jax.random.fold_in(rng, 6), position), (blocks,), jnp.float32, smallest / len(shards), top_value / len(shards))
        return jnp.repeat(jnp.exp(steps), dims[position] // blocks).reshape((-1,) + (1,) * (len(dims) - position - 1))

    factor_of = one(*shards[0])
    for cut in shards[1:]:
        factor_of = factor_of * one(*cut)
    return factor_of


def deal_out(stream_key, own, number, rows, count, top, limit, slope):
    ranking = jax.random.permutation(stream_key, count)
    crowded, usual = portions_of(count, rows * top, limit, slope, True), portions_of(count, rows * top, limit, slope, False)
    places = jnp.arange(count)

    def named(tallies, offset_by):
        used = int((tallies > 0).sum())
        fixed = max(1, used // 4)
        shifted = fixed + (places - fixed + offset_by * (used - fixed)) % max(1, count - fixed)
        return jnp.zeros((count,), jnp.int32).at[ranking[jnp.where(places < fixed, places, shifted)]].set(jnp.asarray(tallies, jnp.int32))

    tallies = jnp.where(number % 4 == 0, named(crowded, number // 4), named(usual, number - number // 4 - 1))
    mixed = jax.random.permutation(jax.random.fold_in(own, 3), count)
    giver, taker = mixed[0:count // 2 * 2:2], mixed[1:count // 2 * 2:2]
    margin = jnp.minimum(tallies[giver] - 1, limit - tallies[taker]) // 2
    margin = jnp.where((giver == ranking[0]) | (taker == ranking[0]) | (tallies[taker] == 0), 0, jnp.maximum(margin, 0))
    shifted = jax.random.randint(jax.random.fold_in(own, 4), (count // 2,), 0, 1 << 20) % (margin + 1)
    tallies = tallies.at[giver].add(-shifted).at[taker].add(shifted)
    items = jnp.searchsorted(jnp.cumsum(tallies), jnp.arange(rows * top), side="right").astype(jnp.int32)
    table = items.reshape(top, rows).T
    table = table[jax.random.permutation(jax.random.fold_in(own, 1), rows)]
    offset_by = jax.random.randint(jax.random.fold_in(own, 2), (rows, 1), 0, top)
    return jnp.take_along_axis(table, (jnp.arange(top)[None, :] + offset_by) % top, axis=1)


def portions_of(amount, total, reach, lean, full):
    portions = [(1 << 20) // math.isqrt(standing ** lean) + 1 for standing in range(1, amount + 1)]
    largest = reach if full else min(reach, max(-(-total // amount), total * portions[0] // sum(portions)))
    least = 1 if total - largest >= amount - 1 else 0
    given, spare = [largest] + [least] * (amount - 1), total - largest - least * (amount - 1)
    while spare > 0:
        free = [i for i in range(1, amount) if given[i] < largest] or [i for i in range(1, amount) if given[i] < reach]
        whole, remaining = sum([portions[i] for i in free]), spare
        for i in free:
            extra = min(reach - given[i], max(1, remaining * portions[i] // whole), spare)
            given[i] = given[i] + extra
            spare = spare - extra
    return np.array(given)


def centred(rng, extent, scale, limit, cuts=(), kind=jnp.bfloat16):
    factor_of = block_levels(rng, extent, cuts, -0.22, 0.18) if cuts else 1.0
    drawn = jax.random.normal(rng, extent, jnp.float32) * scale * factor_of
    return jnp.minimum(jnp.maximum(drawn, -limit), limit).astype(kind)


def setup_inputs(seed: int = 0) -> dict:
    seeds = jax.random.split(jax.random.key(seed), 10)
    velocity = centred(seeds[0], (NX, NY, CZ), 1.0, 6.0, ((0, 8), (1, 64)), jnp.float32)
    rate = jnp.clip(jnp.exp(math.log(0.16) - 2.0794415 * jax.random.uniform(seeds[1], (NX, NY, CZ), jnp.float32) ** block_levels(seeds[1], (NX, NY, CZ), ((0, 8), (1, 64)), -0.2, 0.2)), 0.02, 0.16)
    forcing = centred(seeds[2], (NX, NY, CZ), 0.2, 3.0, ((0, 8), (1, 64)), jnp.float32)
    anchor_line = place_ends(jax.random.randint(seeds[3], (TOTAL,), 0, CX * CY), jax.random.fold_in(seeds[3], 1), 0, (CX * CY) - 1).astype(jnp.int32)
    anchor_z = place_ends(jax.random.randint(seeds[4], (TOTAL,), 0, CZ - SUB + 1), jax.random.fold_in(seeds[4], 1), 0, CZ - SUB).astype(jnp.int32)
    assign_keys = jax.random.split(jax.random.fold_in(seeds[5], 1), TOTAL // ROWS)
    assign_turns = jax.random.permutation(jax.random.fold_in(seeds[5], 3), TOTAL // ROWS)
    assign = jax.vmap(lambda own, number: deal_out(jax.random.fold_in(seeds[5], 2), own, number, ROWS, N_SLAB, 1, CAP, 2))(assign_keys, assign_turns).reshape((TOTAL, 1))
    spectral = centred(seeds[6], (2 * MODES * WIDTH, WIDTH), WIDTH ** -0.5, 0.75, (), jnp.float32)
    dense = centred(seeds[7], (WIDTH + 4, WIDTH), 0.3, 4.0, (), jnp.float32)
    momentum = centred(seeds[8], (2 * MODES * WIDTH, WIDTH), 0.02, 0.3125, ((0, 512),), jnp.float32)
    return dict(velocity=velocity, rate=rate, forcing=forcing, anchor_line=anchor_line, anchor_z=anchor_z, assign=assign, spectral=spectral, dense=dense, momentum=momentum)


decay_rate = 0.9
learn_rate = 0.5
dense_rate = 3.0

def tendency_of(field_now, rate, forcing):
    padded = jnp.pad(field_now, ((1, 1), (1, 1), (0, 0)))
    beside = padded[2:, 1:-1] + padded[:-2, 1:-1] + padded[1:-1, 2:] + padded[1:-1, :-2]
    beside = beside + jnp.roll(field_now, 1, 2) + jnp.roll(field_now, -1, 2)
    return rate * (beside - 6.0 * field_now) + forcing

def tables():
    counts = jnp.arange(SUB, dtype=jnp.int32)
    waves = jnp.arange(MODES, dtype=jnp.int32)
    phase = counts[:, None] * waves[None, :] % SUB
    angle = phase.astype(jnp.float32) * (2.0 * jnp.pi / SUB)
    weight_k = jnp.where(waves == 0, 1.0, 2.0).astype(jnp.float32) / SUB
    return (jnp.cos(angle), jnp.sin(angle), weight_k)

def line_errors(spectral, dense, inputs, targets, valid):
    highest = lax.Precision.HIGHEST
    width = dense.shape[1]
    mixing = dense[:width]
    lift_gain, lift_bias, layer_bias, projection = (dense[width], dense[width + 1], dense[width + 2], dense[width + 3])
    cosine, sine, weight_k = tables()
    hidden = inputs[:, None, :] * lift_gain[None, :, None] + lift_bias[None, :, None]
    real_in = jnp.einsum('bws,sk->bwk', hidden, cosine, precision=highest)
    imag_in = -jnp.einsum('bws,sk->bwk', hidden, sine, precision=highest)
    blocks = spectral.reshape(2, MODES, width, width)
    w_real, w_imag = (blocks[0], blocks[1])
    real_out = jnp.einsum('bwk,kwv->bvk', real_in, w_real, precision=highest) - jnp.einsum('bwk,kwv->bvk', imag_in, w_imag, precision=highest)
    imag_out = jnp.einsum('bwk,kwv->bvk', real_in, w_imag, precision=highest) + jnp.einsum('bwk,kwv->bvk', imag_in, w_real, precision=highest)
    spatial = jnp.einsum('bvk,sk->bvs', real_out * weight_k, cosine, precision=highest) - jnp.einsum('bvk,sk->bvs', imag_out * weight_k, sine, precision=highest)
    before = spatial + jnp.einsum('bws,wv->bvs', hidden, mixing, precision=highest) + layer_bias[None, :, None]
    after = jax.nn.gelu(before)
    output = jnp.einsum('bvs,v->bs', after, projection, precision=highest)
    return lax.optimization_barrier(jnp.sum((output - targets) ** 2, axis=1)) * valid

def reference(velocity, rate, forcing, anchor_line, anchor_z, assign, spectral, dense, momentum):
    field_now = velocity
    previous = velocity
    change = velocity
    for number in range(STEPS):
        previous = field_now
        change = tendency_of(field_now, rate, forcing)
        field_now = field_now + change
    lines = jnp.arange(TOTAL, dtype=jnp.int32)
    device = lines // ROWS
    grp_index = device // N_SLAB
    slab_index = device % N_SLAB
    first = grp_index * CX + anchor_line // CY
    second = slab_index * CY + anchor_line % CY
    windows = jax.vmap(lambda row, start: lax.dynamic_slice_in_dim(row, start, SUB))
    inputs = windows(previous[first, second], anchor_z.astype(jnp.int32))
    targets = windows(change[first, second], anchor_z.astype(jnp.int32))
    scale = 1.0 / (TOTAL * SUB)
    devices = TOTAL // ROWS
    inputs = inputs.reshape(devices, ROWS, SUB)
    targets = targets.reshape(devices, ROWS, SUB)

    def one_block(carry, pieces):
        block_in, block_tg = pieces

        def loss_fn(spec, dens):
            errors = line_errors(spec, dens, block_in, block_tg, jnp.ones((ROWS,), jnp.float32))
            return (jnp.sum(errors) * scale, errors)
        value, pullback, errors = jax.vjp(loss_fn, spectral, dense, has_aux=True)
        grad_spec, grad_dense = pullback(jnp.ones((), jnp.float32))
        return ((carry[0] + grad_spec, carry[1] + grad_dense), errors)
    start = (jnp.zeros_like(spectral), jnp.zeros_like(dense))
    (grad_spec, grad_dense), errors = lax.scan(one_block, start, (inputs, targets))
    errors = errors.reshape(TOTAL)
    trainer = grp_index * N_SLAB + assign[:, 0]
    onehot = (trainer[:, None] == jnp.arange(N_GRP * N_SLAB, dtype=jnp.int32)[None, :]).astype(jnp.float32)
    trainer_loss = jnp.dot(errors, onehot, precision=lax.Precision.HIGHEST) / (ROWS * SUB)
    momentum_new = decay_rate * momentum + grad_spec
    spectral_new = spectral - learn_rate * momentum_new
    dense_new = dense - dense_rate * grad_dense
    return (field_now, trainer_loss.reshape(N_GRP, N_SLAB), spectral_new, dense_new, momentum_new)
```

```python
import jax
import jax.numpy as jnp
import numpy as np
from jax import lax
from jax.experimental import pallas as pl
from jax.experimental.pallas import tpu as pltpu
from jax.sharding import PartitionSpec as P

SUB = 128
MODES = 16
WIDTH = 64
LINES = 16
NG = 8
NS = 64
NZ = 16
PEERS = 32
TOTAL = 8192

decay_rate = 0.9
learn_rate = 0.5
dense_rate = 3.0

MESH = pl.DeviceIdType.MESH
F32 = jnp.float32
HIGHEST = lax.Precision.HIGHEST
GELU_C = float(np.sqrt(2.0 / np.pi))

LANE_P = 0
LANE_M1 = 32
LANE_Q = 40
LANE_M0 = 72
LANE_PROJ = 80
LANE_LOSS = 88


def tables():
    s = np.arange(SUB)[None, :]
    k = np.arange(MODES)[:, None]
    angle = (k * s % SUB) * (2.0 * np.pi / SUB)
    cos, sin = np.cos(angle), np.sin(angle)
    weight = np.where(k == 0, 1.0, 2.0) / SUB
    er, ei = cos.sum(1, keepdims=True), -sin.sum(1, keepdims=True)
    a0 = weight * (er * cos - ei * sin)
    b0 = -weight * (ei * cos + er * sin)
    tail = np.zeros((8, SUB))
    tail[0] = 1.0
    return np.concatenate([cos, -sin, weight * cos, weight * sin, a0, b0, tail]).astype(np.float32)


def nt(a, b):
    return lax.dot_general(a, b, (((1,), (1,)), ((), ())), precision=HIGHEST, preferred_element_type=F32)


def nn(a, b):
    return lax.dot_general(a, b, (((1,), (0,)), ((), ())), precision=HIGHEST, preferred_element_type=F32)


def iota(shape, dim):
    return lax.broadcasted_iota(jnp.int32, shape, dim)


def take_lanes(x, index):
    return jnp.take_along_axis(x, index, axis=1, mode="promise_in_bounds")


def stencil(mid, others, rate, forc):
    beside = others[0] + others[1] + others[2] + others[3]
    beside = beside + pltpu.roll(mid, 1, axis=1) + pltpu.roll(mid, mid.shape[1] - 1, axis=1)
    return rate * (beside - 6.0 * mid) + forc


def kernel(
    vel, rate, forc, aline, az, assign, spec, dense, mom, tab,
    field_o, loss_o, spec_o, dense_o, mom_o,
    vel_v, rate_v, forc_v, asg_v, spec_v, dense_v, tab_v,
    side_snd, side_rcv, corn_snd, corn_rcv,
    v1_s, chg_s, fld_s, samp, diff_s, right, dp_s,
    pairb, zb, bun, gath, base_s, grad_s, out_s, dout_s, mout_s, lout_s,
    pay, rsb, zrb, agb,
    ld, st, ssem, rsem,
):
    g = lax.axis_index("grp")
    s = lax.axis_index("slab")
    z = s // 4
    xc = lax.rem(s, 4)
    xh = xc // 2
    c = lax.rem(xc, 2)
    me = g * 4 + xc
    xy = g * 2 + xh
    d = g * NS + s

    barrier = pltpu.get_barrier_semaphore()

    def greet(device):
        pl.semaphore_signal(barrier, inc=1, device_id=device, device_id_type=MESH)

    def plane_peer(i):
        p = lax.rem(me + i, PEERS)
        return p, (p // 4, z * 4 + lax.rem(p, 4))

    def z_peer(i):
        zz = lax.rem(z + i, NZ)
        return zz, (g, zz * 4 + xc)

    def xy_peer(i):
        p = lax.rem(xy + i, 16)
        return p, (p // 2, z * 4 + lax.rem(p, 2) * 2 + c)

    up_g, dn_g = lax.rem(g + 1, NG), lax.rem(g + NG - 1, NG)
    up_s, dn_s = lax.rem(s + 1, NS), lax.rem(s + NS - 1, NS)
    sides = [(up_g, s), (dn_g, s), (g, up_s), (g, dn_s)]
    corners = [(up_g, up_s), (up_g, dn_s), (dn_g, up_s), (dn_g, dn_s)]
    partner = (g, s + 1 - 2 * c)

    loads = []
    for i, (src, dst) in enumerate(
        [
            (vel, vel_v),
            (rate, rate_v),
            (forc, forc_v),
            (mom, pairb.at[c]),
            (spec, spec_v),
            (dense, dense_v),
            (tab, tab_v),
            (assign, asg_v),
        ]
    ):
        loads.append(pltpu.make_async_copy(src, dst, ld.at[i]))
        loads[-1].start()

    def greet_plane(i, carry):
        greet(plane_peer(i)[1])
        return carry

    def greet_z(i, carry):
        greet(z_peer(i)[1])
        return carry

    for device in sides + corners:
        greet(device)
    lax.fori_loop(1, PEERS, greet_plane, 0)
    lax.fori_loop(1, NZ, greet_z, 0)

    for i in range(4):
        loads[i].wait()

    for n, (a, b) in enumerate([(7, 6), (0, 1)]):
        side_snd[n, 0] = vel_v[a]
        side_snd[n, 1] = vel_v[b]
        side_snd[n, 2] = rate_v[a]
        side_snd[n, 3] = forc_v[a]
        side_snd[2 + n, 0] = vel_v[:, a, :]
        side_snd[2 + n, 1] = vel_v[:, b, :]
        side_snd[2 + n, 2] = rate_v[:, a, :]
        side_snd[2 + n, 3] = forc_v[:, a, :]
    for n, (a, b) in enumerate([(7, 7), (7, 0), (0, 7), (0, 0)]):
        corn_snd[n] = vel_v[a, b : b + 1, :]

    pl.semaphore_wait(barrier, 8 + PEERS - 1 + NZ - 1)

    def send(src, dst, n, device):
        return pltpu.make_async_remote_copy(
            src_ref=src, dst_ref=dst, send_sem=ssem.at[n], recv_sem=rsem.at[n], device_id=device, device_id_type=MESH
        )

    for n in range(4):
        send(side_snd.at[n], side_rcv.at[n], 0, sides[n]).start()
    for n in range(4):
        send(corn_snd.at[n], corn_rcv.at[n], 1, corners[n]).start()
    send(pairb.at[c], pairb.at[c], 2, partner).start()

    for i in range(4, 8):
        loads[i].wait()
    dv = dense_v[...]
    mixing = dv[:, 0:WIDTH]
    eye = iota((WIDTH, WIDTH), 0) == iota((WIDTH, WIDTH), 1)
    gain_row = jnp.sum(jnp.where(eye, dv[:, 64:65], 0.0), axis=0, keepdims=True)
    bias_row = jnp.sum(jnp.where(eye, dv[:, 65:66], 0.0), axis=0, keepdims=True)
    gain_lanes = jnp.concatenate([gain_row, gain_row], axis=1)
    bias_lanes = jnp.concatenate([bias_row, bias_row], axis=1)
    layer_bias = dv[:, 66:67]
    proj = dv[:, 67:68]
    m1 = jnp.sum(mixing * gain_row, axis=1, keepdims=True)
    m0 = jnp.sum(mixing * bias_row, axis=1, keepdims=True) + layer_bias
    weights = spec_v[...]
    segment = jnp.where(iota((40, 2048), 1) // WIDTH == iota((40, 2048), 0), 1.0, 0.0)
    gain_tiled = jnp.concatenate([gain_lanes] * 16, axis=1)
    bias_tiled = jnp.concatenate([bias_lanes] * 16, axis=1)
    lane40 = iota((WIDTH, 40), 1)
    left1 = jnp.where(lane40 == LANE_M1, m1, nt(weights * gain_tiled, segment))
    left0 = jnp.where(lane40 == LANE_M1, m0, nt(weights * bias_tiled, segment))
    left = jnp.concatenate([left1, left0], axis=1)

    send(pairb.at[1 - c], pairb.at[1 - c], 2, partner).wait_recv()
    zb[z] = jnp.concatenate([pairb[0], pairb[1]], axis=0)

    def send_z(i, carry):
        send(zb.at[z], zb.at[z], 3, z_peer(i)[1]).start()
        return carry

    lax.fori_loop(1, NZ, send_z, 0)

    right[32:40, :] = jnp.zeros((8, 2048), F32)
    for t in range(LINES):
        right[40:80, SUB * t : SUB * (t + 1)] = tab_v[64:104, :]

    send(side_snd, side_rcv, 0, partner).wait_recv()
    send(corn_snd, corn_rcv, 1, partner).wait_recv()
    has = [g > 0, g < NG - 1, s > 0, s < NS - 1]
    planes = [[jnp.where(has[n], side_rcv[n, i], 0.0) for i in range(4)] for n in range(4)]
    corner = [
        jnp.where(jnp.logical_and(has[a], has[b]), corn_rcv[n], 0.0)
        for n, (a, b) in enumerate([(0, 2), (0, 3), (1, 2), (1, 3)])
    ]
    row = iota((8, 512), 0)

    def shifted(plane, before, after):
        lo = jnp.where(row == 0, before, pltpu.roll(plane, 1, axis=0))
        hi = jnp.where(row == 7, after, pltpu.roll(plane, 7, axis=0))
        return lo, hi

    ring = []
    for n in range(4):
        mid, far, r, f = planes[n]
        if n == 0:
            ends, own = (corner[0], corner[1]), vel_v[0]
        elif n == 1:
            ends, own = (corner[2], corner[3]), vel_v[7]
        elif n == 2:
            ends, own = (corner[0], corner[2]), vel_v[:, 0, :]
        else:
            ends, own = (corner[1], corner[3]), vel_v[:, 7, :]
        lo, hi = shifted(mid, *ends)
        ring.append(mid + stencil(mid, (far, own, lo, hi), r, f))

    def flow(cells, edge, x):
        mid = cells[x]
        below = edge[0] if x == 0 else cells[x - 1]
        above = edge[1] if x == 7 else cells[x + 1]
        lo, hi = shifted(mid, edge[2][x : x + 1, :], edge[3][x : x + 1, :])
        return mid, stencil(mid, (above, below, hi, lo), rate_v[x], forc_v[x])

    first = [vel_v[x] for x in range(8)]
    edge0 = [planes[n][0] for n in range(4)]
    second = []
    for x in range(8):
        mid, change = flow(first, edge0, x)
        second.append(mid + change)
        v1_s[8 * x : 8 * x + 8, :] = second[x]
    for x in range(8):
        mid, change = flow(second, ring, x)
        chg_s[8 * x : 8 * x + 8, :] = change
        fld_s[x] = mid + change
    field_copy = pltpu.make_async_copy(fld_s, field_o, st.at[0])
    field_copy.start()

    def wait_many(buf, count, n):
        send(buf.at[pl.ds(0, count)], buf.at[pl.ds(0, count)], n, partner).wait_recv()

    wait_many(zb, NZ - 1, 3)
    bun[...] = zb[...].reshape(128, WIDTH).T
    gath[c, xy] = bun[pl.ds(pl.multiple_of(c * 32, 32), 32), :]

    def send_xy(i, carry):
        send(gath.at[c, xy], gath.at[c, xy], 4, xy_peer(i)[1]).start()
        return carry

    lax.fori_loop(1, 16, send_xy, 0)

    row16 = iota((8, SUB), 0)
    for t in range(LINES):
        line = aline[t]
        samp[t : t + 1, :] = v1_s[pl.ds(line, 1), :]
        samp[LINES + t : LINES + t + 1, :] = chg_s[pl.ds(line, 1), :]
    windows = []
    for tile in range(4):
        start = jnp.zeros((8, SUB), jnp.int32)
        for i in range(8):
            start = jnp.where(row16 == i, az[(tile % 2) * 8 + i], start)
        block, shift = start // SUB, start % SUB
        quarter = [samp[8 * tile : 8 * tile + 8, SUB * q : SUB * (q + 1)] for q in range(4)]
        lo = jnp.where(block == 0, quarter[0], jnp.where(block == 1, quarter[1], jnp.where(block == 2, quarter[2], quarter[3])))
        hi = jnp.where(block == 0, quarter[1], jnp.where(block == 1, quarter[2], quarter[3]))
        at = iota((8, SUB), 1) + shift
        index = at % SUB
        windows.append(jnp.where(at < SUB, take_lanes(lo, index), take_lanes(hi, index)))
    inputs = jnp.concatenate(windows[:2], axis=0)
    targets = jnp.concatenate(windows[2:], axis=0)

    spectrum = nt(tab_v[0:32, :], inputs)
    cos_w, sin_w = tab_v[32:48, :], tab_v[48:64, :]
    scale = 1.0 / (TOTAL * SUB)
    proj_grad = jnp.zeros((WIDTH, SUB), F32)
    for pair in range(LINES // 2):
        cols = slice(2 * SUB * pair, 2 * SUB * (pair + 1))
        for half in range(2):
            t = 2 * pair + half
            one = slice(SUB * t, SUB * (t + 1))
            ur, ui = spectrum[0:16, t : t + 1], spectrum[16:32, t : t + 1]
            right[0:16, one] = ur * cos_w - ui * sin_w
            right[16:32, one] = -(ui * cos_w + ur * sin_w)
            right[32:33, one] = inputs[t : t + 1, :]
        pre = nn(left, right[:, cols])
        square = pre * pre
        bend = jnp.tanh(GELU_C * (pre + 0.044715 * (square * pre)))
        half_up = 0.5 * (1.0 + bend)
        hidden = pre * half_up
        slope = half_up + 0.5 * pre * (1.0 - bend * bend) * (GELU_C * (1.0 + 3.0 * 0.044715 * square))
        guess = jnp.sum(hidden * proj, axis=0, keepdims=True)
        target = jnp.concatenate([targets[2 * pair : 2 * pair + 1, :], targets[2 * pair + 1 : 2 * pair + 2, :]], axis=1)
        miss = guess - target
        diff_s[2 * pair : 2 * pair + 1, :] = miss[:, 0:SUB]
        diff_s[2 * pair + 1 : 2 * pair + 2, :] = miss[:, SUB:]
        dq = (2.0 * scale) * miss
        dpre = slope * proj * dq
        dp_s[:, cols] = dpre
        back = hidden * dq
        proj_grad = proj_grad + back[:, 0:SUB] + back[:, SUB:]
    grads = nt(dp_s[...], right[...])

    diff = diff_s[...]
    err = jnp.sum(diff * diff, axis=1, keepdims=True)
    eye16 = iota((LINES, LINES), 0) == iota((LINES, LINES), 1)
    err_row = jnp.sum(jnp.where(eye16, err, 0.0), axis=0, keepdims=True)
    named = iota((NS, LINES), 0) == asg_v[...]
    loss = jnp.sum(jnp.where(named, err_row, 0.0), axis=1, keepdims=True) / (LINES * SUB)

    lane48 = iota((WIDTH, 48), 1)
    extra = jnp.where(lane48 == LANE_PROJ - 80, jnp.sum(proj_grad, axis=1, keepdims=True), 0.0)
    extra = jnp.where(lane48 == LANE_LOSS - 80 + g, loss, extra)
    payload = jnp.concatenate([grads, extra], axis=1)
    for p in range(PEERS):
        pay[p] = payload[2 * p : 2 * p + 2, :]

    def send_scatter(i, carry):
        p, device = plane_peer(i)
        send(pay.at[p], rsb.at[me], 5, device).start()
        return carry

    lax.fori_loop(1, PEERS, send_scatter, 0)
    rsb[me] = pay[me]

    wait_many(gath.at[c], 15, 4)
    send(gath.at[c], gath.at[c], 8, partner).start()

    wait_many(rsb, PEERS - 1, 5)
    zrb[z] = jnp.sum(rsb[...], axis=0)

    def send_line(i, carry):
        send(zrb.at[z], zrb.at[z], 6, z_peer(i)[1]).start()
        return carry

    lax.fori_loop(1, NZ, send_line, 0)

    send(gath.at[1 - c], gath.at[1 - c], 8, partner).wait_recv()
    lane = iota((WIDTH, SUB), 1)
    for j in range(16):
        cols = slice(SUB * j, SUB * (j + 1))
        index = (j % 2) * 64 + (lane // 16) * 8 + lane % 8
        both = [
            take_lanes(jnp.concatenate([gath[0, (j // 2) * 2 + h], gath[1, (j // 2) * 2 + h]], axis=0), index)
            for h in range(2)
        ]
        moved = jnp.where((lane // 8) % 2 == 0, both[0], both[1])
        base_s[:, cols] = spec_v[:, cols] - (learn_rate * decay_rate) * moved

    wait_many(zrb, NZ - 1, 6)
    agb[me] = jnp.sum(zrb[...], axis=0)

    def send_gather(i, carry):
        send(agb.at[me], agb.at[me], 7, plane_peer(i)[1]).start()
        return carry

    lax.fori_loop(1, PEERS, send_gather, 0)
    wait_many(agb, PEERS - 1, 7)
    total = jnp.concatenate([agb[p] for p in range(PEERS)], axis=0)

    gain_back = jnp.zeros((WIDTH, SUB), F32)
    bias_back = jnp.zeros((WIDTH, SUB), F32)
    stores = []
    for j in range(16):
        cols = slice(SUB * j, SUB * (j + 1))
        index = jnp.where(lane < 64, 2 * j, 2 * j + 1)
        by_gain = take_lanes(total, index + LANE_P)
        by_bias = take_lanes(total, index + LANE_Q)
        grad = gain_lanes * by_gain + bias_lanes * by_bias
        grad_s[:, cols] = grad
        out_s[:, cols] = base_s[:, cols] - learn_rate * grad
        w = spec_v[:, cols]
        gain_back = gain_back + by_gain * w
        bias_back = bias_back + by_bias * w
        if j % 4 == 3:
            some = pl.ds(SUB * (j - 3), SUB * 4)
            stores.append(pltpu.make_async_copy(out_s.at[:, some], spec_o.at[:, some], st.at[1 + j // 4]))
            stores[-1].start()

    dm1, dm0 = total[:, LANE_M1 : LANE_M1 + 1], total[:, LANE_M0 : LANE_M0 + 1]

    def to_column(back, dm):
        both = jnp.sum(back, axis=0, keepdims=True)
        both = both[:, 0:WIDTH] + both[:, WIDTH:] + jnp.sum(mixing * dm, axis=0, keepdims=True)
        return jnp.sum(jnp.where(eye, both, 0.0), axis=1, keepdims=True)

    dout_s[:, 0:64] = mixing - dense_rate * (gain_row * dm1 + bias_row * dm0)
    dout_s[:, 64:65] = dv[:, 64:65] - dense_rate * to_column(gain_back, dm1)
    dout_s[:, 65:66] = dv[:, 65:66] - dense_rate * to_column(bias_back, dm0)
    dout_s[:, 66:67] = layer_bias - dense_rate * dm0
    dout_s[:, 67:68] = proj - dense_rate * total[:, LANE_PROJ : LANE_PROJ + 1]
    stores.append(pltpu.make_async_copy(dout_s, dense_o, st.at[5]))
    stores[-1].start()

    mine = grad_s[:, pl.ds(pl.multiple_of((d // 32) * SUB, SUB), SUB)]
    mine = pltpu.roll(mine, lax.rem(SUB - lax.rem(d, 32) * 4, SUB), axis=1)
    mout_s[...] = decay_rate * pairb[c] + mine.T[0:4, :]
    stores.append(pltpu.make_async_copy(mout_s, mom_o, st.at[6]))
    stores[-1].start()

    own = jnp.logical_and(iota((NS, SUB), 0) == s, lane == LANE_LOSS + g)
    own = jnp.sum(jnp.where(own, total, 0.0), axis=1, keepdims=True)
    lout_s[...] = jnp.sum(own, axis=0, keepdims=True)
    stores.append(pltpu.make_async_copy(lout_s, loss_o, st.at[7]))
    stores[-1].start()

    field_copy.wait()
    for copy in stores:
        copy.wait()
    send(side_snd, side_rcv, 0, partner).wait_send()
    send(corn_snd, corn_rcv, 1, partner).wait_send()
    send(pairb.at[c], pairb.at[c], 2, partner).wait_send()

    def sent(buf, count, n):
        send(buf.at[pl.ds(0, count)], buf.at[pl.ds(0, count)], n, partner).wait_send()

    sent(zb, NZ - 1, 3)
    sent(gath.at[c], 15, 4)
    sent(pay, PEERS - 1, 5)
    sent(zrb, NZ - 1, 6)
    sent(agb, PEERS - 1, 7)
    send(gath.at[c], gath.at[c], 8, partner).wait_send()


def local(velocity, rate, forcing, anchor_line, anchor_z, assign, spectral, dense, momentum):
    smem = pl.BlockSpec(memory_space=pltpu.SMEM)
    anyw = pl.BlockSpec(memory_space=pl.ANY)
    vmem = pltpu.VMEM
    field, loss, spec, dens, mom = pl.pallas_call(
        kernel,
        out_shape=(
            jax.ShapeDtypeStruct((8, 8, 512), F32),
            jax.ShapeDtypeStruct((1, 1), F32),
            jax.ShapeDtypeStruct((WIDTH, 2048), F32),
            jax.ShapeDtypeStruct((WIDTH, 68), F32),
            jax.ShapeDtypeStruct((4, WIDTH), F32),
        ),
        in_specs=[anyw, anyw, anyw, smem, smem, anyw, anyw, anyw, anyw, anyw],
        out_specs=(anyw, anyw, anyw, anyw, anyw),
        scratch_shapes=[
            vmem((8, 8, 512), F32),
            vmem((8, 8, 512), F32),
            vmem((8, 8, 512), F32),
            vmem((1, LINES), jnp.int32),
            vmem((WIDTH, 2048), F32),
            vmem((WIDTH, 68), F32),
            vmem((104, SUB), F32),
            vmem((4, 4, 8, 512), F32),
            vmem((4, 4, 8, 512), F32),
            vmem((4, 1, 512), F32),
            vmem((4, 1, 512), F32),
            vmem((64, 512), F32),
            vmem((64, 512), F32),
            vmem((8, 8, 512), F32),
            vmem((2 * LINES, 512), F32),
            vmem((LINES, SUB), F32),
            vmem((80, 2048), F32),
            vmem((WIDTH, 2048), F32),
            vmem((2, 4, WIDTH), F32),
            vmem((NZ, 8, WIDTH), F32),
            vmem((WIDTH, SUB), F32),
            vmem((2, 16, 32, SUB), F32),
            vmem((WIDTH, 2048), F32),
            vmem((WIDTH, 2048), F32),
            vmem((WIDTH, 2048), F32),
            vmem((WIDTH, 68), F32),
            vmem((4, WIDTH), F32),
            vmem((1, 1), F32),
            vmem((PEERS, 2, SUB), F32),
            vmem((PEERS, 2, SUB), F32),
            vmem((NZ, 2, SUB), F32),
            vmem((PEERS, 2, SUB), F32),
            pltpu.SemaphoreType.DMA((8,)),
            pltpu.SemaphoreType.DMA((8,)),
            pltpu.SemaphoreType.DMA((9,)),
            pltpu.SemaphoreType.DMA((9,)),
        ],
        compiler_params=pltpu.CompilerParams(
            collective_id=0, has_side_effects=True, vmem_limit_bytes=32 * 1024 * 1024
        ),
    )(velocity, rate, forcing, anchor_line, anchor_z, assign.T, spectral.T, dense.T, momentum, jnp.asarray(tables()))
    return (field, loss, spec.T, dens.T, mom)


def solution(mesh):
    placed = (
        P("grp", "slab", None),
        P("grp", "slab", None),
        P("grp", "slab", None),
        P(("grp", "slab")),
        P(("grp", "slab")),
        P(("grp", "slab"), None),
        P(),
        P(),
        P(("grp", "slab"), None),
    )
    return jax.shard_map(
        local,
        mesh=mesh,
        in_specs=placed,
        out_specs=(P("grp", "slab", None), P("grp", "slab"), P(), P(), P(("grp", "slab"), None)),
        check_vma=False,
    )
```

```python
import jax
import jax.numpy as jnp
import numpy as np
from jax import lax
from jax.experimental import pallas as pl
from jax.experimental.pallas import tpu as pltpu
from jax.sharding import PartitionSpec as P

SUB = 128
MODES = 16
WIDTH = 64
LINES = 16
NG = 8
NS = 64
NZ = 16
NXY = 16
TOTAL = 8192

decay_rate = 0.9
learn_rate = 0.5
dense_rate = 3.0

MESH = pl.DeviceIdType.MESH
F32 = jnp.float32
BF16 = jnp.bfloat16
HIGHEST = lax.Precision.HIGHEST
GELU_C = float(np.sqrt(2.0 / np.pi))

LANE_P = 0
LANE_Q = 32
LANE_M1 = 64
LANE_M0 = 65
LANE_PROJ = 66
LANE_LOSS = 72
KEEP = 80


def tables():
    s = np.arange(SUB)[None, :]
    k = np.arange(MODES)[:, None]
    angle = (k * s % SUB) * (2.0 * np.pi / SUB)
    cos, sin = np.cos(angle), np.sin(angle)
    weight = np.where(k == 0, 1.0, 2.0) / SUB
    er, ei = cos.sum(1, keepdims=True), -sin.sum(1, keepdims=True)
    a0 = weight * (er * cos - ei * sin)
    b0 = -weight * (ei * cos + er * sin)
    return np.concatenate([cos, -sin, weight * cos, weight * sin, a0, b0]).astype(np.float32)


def nt(a, b, precision=None):
    return lax.dot_general(a, b, (((1,), (1,)), ((), ())), precision=precision, preferred_element_type=F32)


def nn(a, b):
    return lax.dot_general(a, b, (((1,), (0,)), ((), ())), preferred_element_type=F32)


def parts(x):
    high = x.astype(BF16)
    return high, (x - high.astype(F32)).astype(BF16)


def iota(shape, dim):
    return lax.broadcasted_iota(jnp.int32, shape, dim)


def take_lanes(x, index):
    return jnp.take_along_axis(x, index, axis=1, mode="promise_in_bounds")


def stencil(mid, others, rate, forc):
    beside = others[0] + others[1] + others[2] + others[3]
    beside = beside + pltpu.roll(mid, 1, axis=1) + pltpu.roll(mid, mid.shape[1] - 1, axis=1)
    return rate * (beside - 6.0 * mid) + forc


def kernel(
    vel, rate, forc, aline, az, assign, spec, dense, mom, tab,
    field_o, loss_o, spec_o, dense_o, mom_o,
    vel_v, rate_v, forc_v, asg_v, spec_v, dense_v, tab_v,
    edge_snd, edge_rcv,
    v1_s, chg_s, samp, diff_s, right, dp_s,
    mz, gath, base_s, grad_s,
    pay, crs, half_s, rsb, zrb, agb,
    ld, ssem, rsem,
):
    g = lax.axis_index("grp")
    s = lax.axis_index("slab")
    z = s // 4
    xc = lax.rem(s, 4)
    xh = xc // 2
    c = lax.rem(xc, 2)
    xy = g * 2 + xh
    d = g * NS + s

    barrier = pltpu.get_barrier_semaphore()

    def greet(device):
        pl.semaphore_signal(barrier, inc=1, device_id=device, device_id_type=MESH)

    def z_peer(i):
        zz = lax.rem(z + i, NZ)
        return (g, zz * 4 + xc)

    def xy_peer(i):
        p = lax.rem(xy + i, NXY)
        return p, (p // 2, z * 4 + lax.rem(p, 2) * 2 + c)

    sides = [
        (lax.rem(g + 1, NG), s),
        (lax.rem(g + NG - 1, NG), s),
        (g, lax.rem(s + 1, NS)),
        (g, lax.rem(s + NS - 1, NS)),
    ]
    partner = (g, s + 1 - 2 * c)

    def load(src, dst, n):
        copy = pltpu.make_async_copy(src, dst, ld.at[n])
        copy.start()
        return copy

    def greet_z(i, carry):
        greet(z_peer(i))
        return carry

    def greet_xy(i, carry):
        greet(xy_peer(i)[1])
        return carry

    vel_load = load(vel, vel_v, 0)
    for device in sides:
        greet(device)
    greet(partner)
    lax.fori_loop(1, NZ, greet_z, 0, unroll=True)
    lax.fori_loop(1, NXY, greet_xy, 0, unroll=True)
    mom_load = load(mom, mz.at[z], 1)
    flow_loads = [load(rate, rate_v, 2), load(forc, forc_v, 3)]
    other_loads = [load(spec, spec_v, 4), load(dense, dense_v, 5), load(tab, tab_v, 6), load(assign, asg_v, 7)]

    def send(src, dst, n, device):
        return pltpu.make_async_remote_copy(
            src_ref=src, dst_ref=dst, send_sem=ssem.at[n], recv_sem=rsem.at[n], device_id=device, device_id_type=MESH
        )

    def arrived(buf, count, n):
        send(buf.at[pl.ds(0, count)], buf.at[pl.ds(0, count)], n, partner).wait_recv()

    def sent(buf, count, n):
        send(buf.at[pl.ds(0, count)], buf.at[pl.ds(0, count)], n, partner).wait_send()

    def send_edges(phase):
        for n in range(4):
            send(edge_snd.at[phase, n], edge_rcv.at[phase, n], phase, sides[n]).start()

    vel_load.wait()
    edge_snd[0, 0] = vel_v[7]
    edge_snd[0, 1] = vel_v[0]
    edge_snd[0, 2] = vel_v[:, 7, :]
    edge_snd[0, 3] = vel_v[:, 0, :]
    pl.semaphore_wait(barrier, 5 + NZ - 1 + NXY - 1)
    send_edges(0)

    mom_load.wait()

    def send_z(i, carry):
        send(mz.at[z], mz.at[z], 2, z_peer(i)).start()
        return carry

    lax.fori_loop(1, NZ, send_z, 0, unroll=True)

    for copy in other_loads:
        copy.wait()
    dv = dense_v[...]
    mixing = dv[:, 0:WIDTH]
    eye = iota((WIDTH, WIDTH), 0) == iota((WIDTH, WIDTH), 1)
    gain_row = jnp.sum(jnp.where(eye, dv[:, 64:65], 0.0), axis=0, keepdims=True)
    bias_row = jnp.sum(jnp.where(eye, dv[:, 65:66], 0.0), axis=0, keepdims=True)
    gain_lanes = jnp.concatenate([gain_row, gain_row], axis=1)
    bias_lanes = jnp.concatenate([bias_row, bias_row], axis=1)
    layer_bias = dv[:, 66:67]
    proj = dv[:, 67:68]
    m1 = jnp.sum(mixing * gain_row, axis=1, keepdims=True)
    m0 = jnp.sum(mixing * bias_row, axis=1, keepdims=True) + layer_bias
    weights = spec_v[...]
    segment = jnp.where(iota((32, 2048), 1) // WIDTH == iota((32, 2048), 0), 1.0, 0.0).astype(BF16)
    gain_high, gain_low = parts(weights * jnp.concatenate([gain_lanes] * 16, axis=1))
    bias_high, bias_low = parts(weights * jnp.concatenate([bias_lanes] * 16, axis=1))
    seen = nt(jnp.concatenate([gain_high, gain_low, bias_high, bias_low], axis=0), segment)
    lane16 = iota((WIDTH, 16), 1)
    left = jnp.concatenate(
        [
            seen[0:64] + seen[64:128],
            seen[128:192] + seen[192:256],
            jnp.where(lane16 == 0, m1, jnp.where(lane16 == 1, m0, 0.0)),
        ],
        axis=1,
    )
    left_high, left_low = parts(left)
    left3 = jnp.concatenate([left_high, left_high, left_low], axis=1)
    for row0, part in zip((32, 112, 192), [parts(tab_v[64:96, :])[i] for i in (0, 1, 0)]):
        for t in range(LINES):
            right[row0 : row0 + 32, SUB * t : SUB * (t + 1)] = part

    has = [g > 0, g < NG - 1, s > 0, s < NS - 1]
    row = iota((8, 512), 0)

    def flow(cells, phase):
        edge = [jnp.where(has[n], edge_rcv[phase, n], 0.0) for n in range(4)]
        changes = []
        for x in range(8):
            mid = cells[x]
            below = edge[0] if x == 0 else cells[x - 1]
            above = edge[1] if x == 7 else cells[x + 1]
            left_of = jnp.where(row == 0, edge[2][x : x + 1, :], pltpu.roll(mid, 1, axis=0))
            right_of = jnp.where(row == 7, edge[3][x : x + 1, :], pltpu.roll(mid, 7, axis=0))
            beside = above + below + right_of + left_of
            beside = beside + pltpu.roll(mid, 1, axis=1) + pltpu.roll(mid, 511, axis=1)
            changes.append(rate_v[x] * (beside - 6.0 * mid) + forc_v[x])
        return changes

    for copy in flow_loads:
        copy.wait()
    arrived(edge_rcv.at[0], 4, 0)
    first = [vel_v[x] for x in range(8)]
    second = [mid + change for mid, change in zip(first, flow(first, 0))]
    edge_snd[1, 0] = second[7]
    edge_snd[1, 1] = second[0]
    edge_snd[1, 2] = jnp.concatenate([p[7:8, :] for p in second], axis=0)
    edge_snd[1, 3] = jnp.concatenate([p[0:1, :] for p in second], axis=0)
    send_edges(1)
    for x in range(8):
        v1_s[8 * x : 8 * x + 8, :] = second[x]

    arrived(mz, NZ - 1, 2)
    turned = jnp.concatenate([mz[i] for i in range(NZ)], axis=0).T
    gath[c, xy] = jnp.concatenate([turned[0:32, :], turned[32:64, :]], axis=1)

    def send_xy(i, carry):
        send(gath.at[c, xy], gath.at[c, xy], 3, xy_peer(i)[1]).start()
        return carry

    lax.fori_loop(1, NXY, send_xy, 0, unroll=True)

    for t in range(LINES):
        samp[t : t + 1, :] = v1_s[pl.ds(aline[t], 1), :]
    row8 = iota((8, SUB), 0)

    def windows(tile):
        start = jnp.zeros((8, SUB), jnp.int32)
        for i in range(8):
            start = jnp.where(row8 == i, az[(tile % 2) * 8 + i], start)
        block, shift = start // SUB, start % SUB
        quarter = [samp[8 * tile : 8 * tile + 8, SUB * q : SUB * (q + 1)] for q in range(4)]
        lo = jnp.where(block == 0, quarter[0], jnp.where(block == 1, quarter[1], jnp.where(block == 2, quarter[2], quarter[3])))
        hi = jnp.where(block == 0, quarter[1], jnp.where(block == 1, quarter[2], quarter[3]))
        at = iota((8, SUB), 1) + shift
        index = at % SUB
        return jnp.where(at < SUB, take_lanes(lo, index), take_lanes(hi, index))

    inputs = jnp.concatenate([windows(0), windows(1)], axis=0)
    spectrum = nt(tab_v[0:32, :], inputs, HIGHEST)
    cos_w, sin_w = tab_v[32:48, :], tab_v[48:64, :]
    row16 = iota((16, SUB), 0)
    for t in range(LINES):
        one = slice(SUB * t, SUB * (t + 1))
        ur, ui = spectrum[0:16, t : t + 1], spectrum[16:32, t : t + 1]
        waves = jnp.concatenate([ur * cos_w - ui * sin_w, -(ui * cos_w + ur * sin_w)], axis=0)
        high, low = parts(waves)
        right[0:32, one] = high
        right[80:112, one] = low
        right[160:192, one] = high
        rest = jnp.where(row16 == 0, inputs[t : t + 1, :], jnp.where(row16 == 1, 1.0, 0.0))
        high, low = parts(rest)
        right[64:80, one] = high
        right[144:160, one] = low
        right[224:240, one] = high

    arrived(edge_rcv.at[1], 4, 1)
    for x, change in enumerate(flow(second, 1)):
        chg_s[8 * x : 8 * x + 8, :] = change
        field_o[x] = second[x] + change
    for t in range(LINES):
        samp[LINES + t : LINES + t + 1, :] = chg_s[pl.ds(aline[t], 1), :]
    targets = jnp.concatenate([windows(2), windows(3)], axis=0)

    scale = 1.0 / (TOTAL * SUB)
    proj_grad = jnp.zeros((WIDTH, SUB), F32)
    for pair in range(LINES // 2):
        cols = slice(2 * SUB * pair, 2 * SUB * (pair + 1))
        pre = nn(left3, right[:, cols])
        square = pre * pre
        bend = jnp.tanh(GELU_C * (pre + 0.044715 * (square * pre)))
        half_up = 0.5 * (1.0 + bend)
        hidden = pre * half_up
        slope = half_up + 0.5 * pre * (1.0 - bend * bend) * (GELU_C * (1.0 + 3.0 * 0.044715 * square))
        guess = jnp.sum(hidden * proj, axis=0, keepdims=True)
        target = jnp.concatenate([targets[2 * pair : 2 * pair + 1, :], targets[2 * pair + 1 : 2 * pair + 2, :]], axis=1)
        miss = guess - target
        diff_s[2 * pair : 2 * pair + 1, :] = miss[:, 0:SUB]
        diff_s[2 * pair + 1 : 2 * pair + 2, :] = miss[:, SUB:]
        dq = (2.0 * scale) * miss
        high, low = parts(slope * proj * dq)
        dp_s[0:64, cols] = high
        dp_s[64:128, cols] = low
        back = hidden * dq
        proj_grad = proj_grad + back[:, 0:SUB] + back[:, SUB:]
    grads = nt(dp_s[...], right[0:160, :])
    grads = grads[0:64, 0:KEEP] + grads[0:64, KEEP:] + grads[64:128, 0:KEEP]

    diff = diff_s[...]
    err = jnp.sum(diff * diff, axis=1, keepdims=True)
    eye16 = iota((LINES, LINES), 0) == iota((LINES, LINES), 1)
    err_row = jnp.sum(jnp.where(eye16, err, 0.0), axis=0, keepdims=True)
    named = iota((NS, LINES), 0) == asg_v[...]
    loss = jnp.sum(jnp.where(named, err_row, 0.0), axis=1, keepdims=True) / (LINES * SUB)

    keep = iota((WIDTH, KEEP), 1)
    grads = jnp.where(keep == LANE_PROJ, jnp.sum(proj_grad, axis=1, keepdims=True), grads)
    grads = jnp.where(keep == LANE_LOSS + g, loss, grads)
    payload = jnp.concatenate([grads, jnp.zeros((WIDTH, SUB - KEEP), F32)], axis=1)
    for h in range(2):
        for p in range(NXY):
            pay[h, p] = payload[32 * h + 2 * p : 32 * h + 2 * p + 2, :]

    send(pay.at[1 - c], crs, 4, partner).start()

    arrived(gath.at[c], NXY - 1, 3)
    send(gath.at[c], gath.at[c], 5, partner).start()

    send(pay.at[1 - c], crs, 4, partner).wait_recv()
    half_s[...] = pay[c] + crs[...]

    def send_scatter(i, carry):
        p, device = xy_peer(i)
        send(half_s.at[p], rsb.at[xy], 6, device).start()
        return carry

    lax.fori_loop(1, NXY, send_scatter, 0, unroll=True)
    rsb[xy] = half_s[xy]
    arrived(rsb, NXY - 1, 6)
    zrb[z] = jnp.sum(rsb[...], axis=0)

    def send_line(i, carry):
        send(zrb.at[z], zrb.at[z], 7, z_peer(i)).start()
        return carry

    lax.fori_loop(1, NZ, send_line, 0, unroll=True)

    send(gath.at[1 - c], gath.at[1 - c], 5, partner).wait_recv()
    lane32 = iota((32, SUB), 1)
    for j in range(16):
        for v in range(2):
            index = v * 64 + ((j % 2) * 8 + lane32 // 16) * 4 + lane32 % 4
            four = [take_lanes(gath[k % 2, (j // 2) * 2 + k // 2], index) for k in range(4)]
            moved = jnp.where(
                (lane32 // 8) % 2 == 0,
                jnp.where((lane32 // 4) % 2 == 0, four[0], four[1]),
                jnp.where((lane32 // 4) % 2 == 0, four[2], four[3]),
            )
            at = (slice(32 * v, 32 * v + 32), slice(SUB * j, SUB * (j + 1)))
            base_s[at] = spec_v[at] - (learn_rate * decay_rate) * moved

    arrived(zrb, NZ - 1, 7)
    agb[c, xy] = jnp.sum(zrb[...], axis=0)

    def send_gather(i, carry):
        send(agb.at[c, xy], agb.at[c, xy], 8, xy_peer(i)[1]).start()
        return carry

    lax.fori_loop(1, NXY, send_gather, 0, unroll=True)
    arrived(agb.at[c], NXY - 1, 8)
    send(agb.at[c], agb.at[c], 9, partner).start()
    send(agb.at[1 - c], agb.at[1 - c], 9, partner).wait_recv()
    total = jnp.concatenate([agb[h, p] for h in range(2) for p in range(NXY)], axis=0)

    lane = iota((WIDTH, SUB), 1)
    gain_back = jnp.zeros((WIDTH, SUB), F32)
    bias_back = jnp.zeros((WIDTH, SUB), F32)
    for j in range(16):
        cols = slice(SUB * j, SUB * (j + 1))
        index = jnp.where(lane < 64, 2 * j, 2 * j + 1)
        by_gain = take_lanes(total, index + LANE_P)
        by_bias = take_lanes(total, index + LANE_Q)
        grad = gain_lanes * by_gain + bias_lanes * by_bias
        grad_s[:, cols] = grad
        spec_o[:, cols] = base_s[:, cols] - learn_rate * grad
        w = spec_v[:, cols]
        gain_back = gain_back + by_gain * w
        bias_back = bias_back + by_bias * w

    dm1, dm0 = total[:, LANE_M1 : LANE_M1 + 1], total[:, LANE_M0 : LANE_M0 + 1]

    def to_column(back, dm):
        both = jnp.sum(back, axis=0, keepdims=True)
        both = both[:, 0:WIDTH] + both[:, WIDTH:] + jnp.sum(mixing * dm, axis=0, keepdims=True)
        return jnp.sum(jnp.where(eye, both, 0.0), axis=1, keepdims=True)

    dense_o[:, 0:64] = mixing - dense_rate * (gain_row * dm1 + bias_row * dm0)
    dense_o[:, 64:65] = dv[:, 64:65] - dense_rate * to_column(gain_back, dm1)
    dense_o[:, 65:66] = dv[:, 65:66] - dense_rate * to_column(bias_back, dm0)
    dense_o[:, 66:67] = layer_bias - dense_rate * dm0
    dense_o[:, 67:68] = proj - dense_rate * total[:, LANE_PROJ : LANE_PROJ + 1]

    mine = grad_s[:, pl.ds(pl.multiple_of((d // 32) * SUB, SUB), SUB)]
    mine = pltpu.roll(mine, lax.rem(SUB - lax.rem(d, 32) * 4, SUB), axis=1)
    mom_o[...] = decay_rate * mz[z] + mine.T[0:4, :]

    own = jnp.logical_and(iota((NS, SUB), 0) == s, lane == LANE_LOSS + g)
    own = jnp.sum(jnp.where(own, total, 0.0), axis=1, keepdims=True)
    loss_o[...] = jnp.sum(own, axis=0, keepdims=True)

    sent(edge_snd.at[0], 4, 0)
    sent(edge_snd.at[1], 4, 1)
    sent(mz, NZ - 1, 2)
    sent(gath.at[c], NXY - 1, 3)
    send(pay.at[1 - c], crs, 4, partner).wait_send()
    send(gath.at[c], gath.at[c], 5, partner).wait_send()
    sent(half_s, NXY - 1, 6)
    sent(zrb, NZ - 1, 7)
    sent(agb.at[c], NXY - 1, 8)
    send(agb.at[c], agb.at[c], 9, partner).wait_send()


def write(*refs):
    sources, results, sems = refs[:5], refs[5:10], refs[10]
    copies = [pltpu.make_async_copy(a, b, sems.at[i]) for i, (a, b) in enumerate(zip(sources, results))]
    for copy in copies:
        copy.start()
    for copy in copies:
        copy.wait()


def local(velocity, rate, forcing, anchor_line, anchor_z, assign, spectral, dense, momentum):
    smem = pl.BlockSpec(memory_space=pltpu.SMEM)
    hbm = pl.BlockSpec(memory_space=pltpu.HBM)
    whole = pl.BlockSpec(memory_space=pltpu.VMEM)
    vmem = pltpu.VMEM
    shapes = (
        jax.ShapeDtypeStruct((8, 8, 512), F32),
        jax.ShapeDtypeStruct((1, 1), F32),
        jax.ShapeDtypeStruct((WIDTH, 2048), F32),
        jax.ShapeDtypeStruct((WIDTH, 68), F32),
        jax.ShapeDtypeStruct((4, WIDTH), F32),
    )

    def pin(x):
        return pltpu.with_memory_space_constraint(x, pltpu.HBM)

    velocity, rate, forcing, momentum = pin(velocity), pin(rate), pin(forcing), pin(momentum)
    anchor_line, anchor_z = pin(anchor_line), pin(anchor_z)
    results = pl.pallas_call(
        kernel,
        out_shape=shapes,
        in_specs=[hbm, hbm, hbm, smem, smem, hbm, hbm, hbm, hbm, hbm],
        out_specs=(whole,) * 5,
        scratch_shapes=[
            vmem((8, 8, 512), F32),
            vmem((8, 8, 512), F32),
            vmem((8, 8, 512), F32),
            vmem((1, LINES), jnp.int32),
            vmem((WIDTH, 2048), F32),
            vmem((WIDTH, 68), F32),
            vmem((96, SUB), F32),
            vmem((2, 4, 8, 512), F32),
            vmem((2, 4, 8, 512), F32),
            vmem((64, 512), F32),
            vmem((64, 512), F32),
            vmem((2 * LINES, 512), F32),
            vmem((LINES, SUB), F32),
            vmem((3 * KEEP, 2048), BF16),
            vmem((2 * WIDTH, 2048), BF16),
            vmem((NZ, 4, WIDTH), F32),
            vmem((2, NXY, 32, SUB), F32),
            vmem((WIDTH, 2048), F32),
            vmem((WIDTH, 2048), F32),
            vmem((2, NXY, 2, SUB), F32),
            vmem((NXY, 2, SUB), F32),
            vmem((NXY, 2, SUB), F32),
            vmem((NXY, 2, SUB), F32),
            vmem((NZ, 2, SUB), F32),
            vmem((2, NXY, 2, SUB), F32),
            pltpu.SemaphoreType.DMA((8,)),
            pltpu.SemaphoreType.DMA((10,)),
            pltpu.SemaphoreType.DMA((10,)),
        ],
        compiler_params=pltpu.CompilerParams(
            collective_id=0, has_side_effects=True, vmem_limit_bytes=32 * 1024 * 1024
        ),
    )(velocity, rate, forcing, anchor_line, anchor_z, pin(assign.T), pin(spectral.T), pin(dense.T), momentum, pin(jnp.asarray(tables())))
    field, loss, spec, dens, mom = pl.pallas_call(
        write,
        out_shape=shapes,
        in_specs=[pl.BlockSpec(memory_space=pl.ANY)] * 5,
        out_specs=(hbm,) * 5,
        scratch_shapes=[pltpu.SemaphoreType.DMA((5,))],
        compiler_params=pltpu.CompilerParams(vmem_limit_bytes=1024 * 1024),
    )(*results)
    return (field, loss, spec.T, dens.T, mom)


def solution(mesh):
    placed = (
        P("grp", "slab", None),
        P("grp", "slab", None),
        P("grp", "slab", None),
        P(("grp", "slab")),
        P(("grp", "slab")),
        P(("grp", "slab"), None),
        P(),
        P(),
        P(("grp", "slab"), None),
    )
    return jax.shard_map(
        local,
        mesh=mesh,
        in_specs=placed,
        out_specs=(P("grp", "slab", None), P("grp", "slab"), P(), P(), P(("grp", "slab"), None)),
        check_vma=False,
    )
```

```python
import jax
import jax.numpy as jnp
import numpy as np
from jax import lax
from jax.experimental import pallas as pl
from jax.experimental.pallas import tpu as pltpu
from jax.sharding import PartitionSpec as P

SUB = 128
MODES = 16
WIDTH = 64
LINES = 16
NG = 8
NS = 64
NZ = 16
NXY = 16
TOTAL = 8192

decay_rate = 0.9
learn_rate = 0.5
dense_rate = 3.0

MESH = pl.DeviceIdType.MESH
F32 = jnp.float32
BF16 = jnp.bfloat16
HIGHEST = lax.Precision.HIGHEST
GELU_C = float(np.sqrt(2.0 / np.pi))

Z_ORDER = (8, 7, 9, 6, 10, 5, 11, 4, 12, 3, 13, 2, 14, 1, 15)
Z_NEAR = (3, 13, 2, 14, 1, 15)
XY_ORDER = tuple(
    sorted(
        ((a, b, c) for a in range(2) for b in range(4) for c in range(2) if a + b + c),
        key=lambda i: -(min(i[1], 4 - i[1]) + (2 * i[2] if not i[0] else 1)),
    )
)
XY_ROW = ((1, 0, 0), (0, 0, 1), (1, 0, 1))
XY_COLUMN = ((0, 1, 0), (0, 2, 0), (0, 3, 0))

LANE_P = 0
LANE_Q = 32
LANE_M1 = 64
LANE_M0 = 65
LANE_PROJ = 66
LANE_LOSS = 72
KEEP = 80


def tables():
    s = np.arange(SUB)[None, :]
    k = np.arange(MODES)[:, None]
    angle = (k * s % SUB) * (2.0 * np.pi / SUB)
    cos, sin = np.cos(angle), np.sin(angle)
    weight = np.where(k == 0, 1.0, 2.0) / SUB
    er, ei = cos.sum(1, keepdims=True), -sin.sum(1, keepdims=True)
    a0 = weight * (er * cos - ei * sin)
    b0 = -weight * (ei * cos + er * sin)
    return np.concatenate([cos, -sin, weight * cos, weight * sin, a0, b0]).astype(np.float32)


def nt(a, b, precision=None):
    return lax.dot_general(a, b, (((1,), (1,)), ((), ())), precision=precision, preferred_element_type=F32)


def nn(a, b):
    return lax.dot_general(a, b, (((1,), (0,)), ((), ())), preferred_element_type=F32)


def parts(x):
    high = x.astype(BF16)
    return high, (x - high.astype(F32)).astype(BF16)


def iota(shape, dim):
    return lax.broadcasted_iota(jnp.int32, shape, dim)


def take_lanes(x, index):
    return jnp.take_along_axis(x, index, axis=1, mode="promise_in_bounds")


def stencil(mid, others, rate, forc):
    beside = others[0] + others[1] + others[2] + others[3]
    beside = beside + pltpu.roll(mid, 1, axis=1) + pltpu.roll(mid, mid.shape[1] - 1, axis=1)
    return rate * (beside - 6.0 * mid) + forc


def kernel(
    vel, rate, forc, aline, az, assign, spec, dense, mom, tab,
    field_o, loss_o, spec_o, dense_o, mom_o,
    vel_v, rate_v, forc_v, asg_v, spec_v, dense_v, tab_v,
    side_snd, side_rcv, corn_snd, corn_rcv,
    v1_s, chg_s, samp, diff_s, right, dp_s,
    mz, gath, base_s, grad_s,
    pay, crs, half_s, rsb, zrb, agb,
    ld, ssem, rsem, know,
):
    g = lax.axis_index("grp")
    s = lax.axis_index("slab")
    z = s // 4
    xc = lax.rem(s, 4)
    xh = xc // 2
    c = lax.rem(xc, 2)
    xy = g * 2 + xh
    d = g * NS + s

    barrier = pltpu.get_barrier_semaphore()

    def greet(device):
        pl.semaphore_signal(barrier, inc=1, device_id=device, device_id_type=MESH)

    xl, y = g // 4, lax.rem(g, 4)

    def z_peer(i):
        return (g, lax.rem(z + i, NZ) * 4 + xc)

    def xy_peer(i):
        flip_l, step, flip_h = i
        gg = (xl + flip_l - 2 * flip_l * xl) * 4 + lax.rem(y + step, 4)
        hh = xh + flip_h - 2 * flip_h * xh
        return gg * 2 + hh, (gg, z * 4 + hh * 2 + c)

    up_g, dn_g = lax.rem(g + 1, NG), lax.rem(g + NG - 1, NG)
    up_s, dn_s = lax.rem(s + 1, NS), lax.rem(s + NS - 1, NS)
    sides = [(up_g, s), (dn_g, s), (g, up_s), (g, dn_s)]
    corners = [(up_g, up_s), (up_g, dn_s), (dn_g, up_s), (dn_g, dn_s)]
    partner = (g, s + 1 - 2 * c)

    near = corners + [z_peer(i) for i in Z_NEAR] + [xy_peer(i)[1] for i in XY_ROW + XY_COLUMN] + sides + [partner]

    def load(src, dst, n):
        copy = pltpu.make_async_copy(src, dst, ld.at[n])
        copy.start()
        return copy

    flow_loads = [load(vel, vel_v, 0), load(rate, rate_v, 2), load(forc, forc_v, 3)]
    for device in near:
        greet(device)
    mom_load = load(mom, mz.at[z], 1)
    other_loads = [load(spec, spec_v, 4), load(dense, dense_v, 5), load(tab, tab_v, 6), load(assign, asg_v, 7)]

    def send(src, dst, n, device):
        return pltpu.make_async_remote_copy(
            src_ref=src, dst_ref=dst, send_sem=ssem.at[n], recv_sem=rsem.at[n], device_id=device, device_id_type=MESH
        )

    def arrived(buf, count, n):
        send(buf.at[pl.ds(0, count)], buf.at[pl.ds(0, count)], n, partner).wait_recv()

    def sent(buf, count, n):
        send(buf.at[pl.ds(0, count)], buf.at[pl.ds(0, count)], n, partner).wait_send()

    def tell(n, device):
        pl.semaphore_signal(know.at[n], inc=1, device_id=device, device_id_type=MESH)

    row = iota((8, 512), 0)

    def shifted(plane, before, after):
        lo = jnp.where(row == 0, before, pltpu.roll(plane, 1, axis=0))
        hi = jnp.where(row == 7, after, pltpu.roll(plane, 7, axis=0))
        return lo + hi

    def along(plane):
        return pltpu.roll(plane, 1, axis=1) + pltpu.roll(plane, 511, axis=1)

    for copy in flow_loads:
        copy.wait()
    for n, (a, b) in enumerate([(7, 6), (0, 1), (7, 6), (0, 1)]):
        pick = (lambda ref, i: ref[i]) if n < 2 else (lambda ref, i: ref[:, i, :])
        mid, far, r, f = pick(vel_v, a), pick(vel_v, b), pick(rate_v, a), pick(forc_v, a)
        side_snd[n, 0] = mid
        side_snd[n, 1] = mid + (r * (far + shifted(mid, 0.0, 0.0) + along(mid) - 6.0 * mid) + f)
        side_snd[n, 2] = r
    for n, (a, b) in enumerate([(7, 7), (7, 0), (0, 7), (0, 0)]):
        corn_snd[n] = vel_v[a, b : b + 1, :]
    pl.semaphore_wait(barrier, len(near))
    for n in range(4):
        send(side_snd.at[n], side_rcv.at[n], 0, sides[n]).start()
    for n in range(4):
        send(corn_snd.at[n], corn_rcv.at[n], 1, corners[n]).start()

    for i in (3, NZ - 3):
        tell(0, z_peer(i))
    for i in XY_COLUMN:
        tell(2, xy_peer(i)[1])

    for copy in other_loads:
        copy.wait()
    dv = dense_v[...]
    mixing = dv[:, 0:WIDTH]
    eye = iota((WIDTH, WIDTH), 0) == iota((WIDTH, WIDTH), 1)
    gain_row = jnp.sum(jnp.where(eye, dv[:, 64:65], 0.0), axis=0, keepdims=True)
    bias_row = jnp.sum(jnp.where(eye, dv[:, 65:66], 0.0), axis=0, keepdims=True)
    gain_lanes = jnp.concatenate([gain_row, gain_row], axis=1)
    bias_lanes = jnp.concatenate([bias_row, bias_row], axis=1)
    layer_bias = dv[:, 66:67]
    proj = dv[:, 67:68]
    m1 = jnp.sum(mixing * gain_row, axis=1, keepdims=True)
    m0 = jnp.sum(mixing * bias_row, axis=1, keepdims=True) + layer_bias
    weights = spec_v[...]
    segment = jnp.where(iota((32, 2048), 1) // WIDTH == iota((32, 2048), 0), 1.0, 0.0).astype(BF16)
    gain_high, gain_low = parts(weights * jnp.concatenate([gain_lanes] * 16, axis=1))
    bias_high, bias_low = parts(weights * jnp.concatenate([bias_lanes] * 16, axis=1))
    seen = nt(jnp.concatenate([gain_high, gain_low, bias_high, bias_low], axis=0), segment)
    lane16 = iota((WIDTH, 16), 1)
    left = jnp.concatenate(
        [
            seen[0:64] + seen[64:128],
            seen[128:192] + seen[192:256],
            jnp.where(lane16 == 0, m1, jnp.where(lane16 == 1, m0, 0.0)),
        ],
        axis=1,
    )
    left_high, left_low = parts(left)
    left3 = jnp.concatenate([left_high, left_high, left_low], axis=1)
    for row0, part in zip((32, 112, 192), [parts(tab_v[64:96, :])[i] for i in (0, 1, 0)]):
        for t in range(LINES):
            right[row0 : row0 + 32, SUB * t : SUB * (t + 1)] = part

    pl.semaphore_wait(know.at[0], 2)
    for i in (2, NZ - 2):
        tell(1, z_peer(i))

    send(side_snd, side_rcv, 0, partner).wait_recv()
    send(corn_snd, corn_rcv, 1, partner).wait_recv()
    has = [g > 0, g < NG - 1, s > 0, s < NS - 1]
    corner = [
        jnp.where(jnp.logical_and(has[a], has[b]), corn_rcv[n], 0.0)
        for n, (a, b) in enumerate([(0, 2), (0, 3), (1, 2), (1, 3)])
    ]
    edge0, edge1 = [], []
    for n, (a, lo, hi) in enumerate([(0, 0, 1), (7, 2, 3), (0, 0, 2), (7, 1, 3)]):
        mid, part, r = [jnp.where(has[n], side_rcv[n, i], 0.0) for i in range(3)]
        own = vel_v[a] if n < 2 else vel_v[:, a, :]
        ends = jnp.where(row == 0, corner[lo], jnp.where(row == 7, corner[hi], 0.0))
        edge0.append(mid)
        edge1.append(part + r * (own + ends))

    def flow(cells, edge):
        changes = []
        for x in range(8):
            mid = cells[x]
            below = edge[0] if x == 0 else cells[x - 1]
            above = edge[1] if x == 7 else cells[x + 1]
            beside = above + below + shifted(mid, edge[2][x : x + 1, :], edge[3][x : x + 1, :]) + along(mid)
            changes.append(rate_v[x] * (beside - 6.0 * mid) + forc_v[x])
        return changes

    first = [vel_v[x] for x in range(8)]
    second = [mid + change for mid, change in zip(first, flow(first, edge0))]
    for x in range(8):
        v1_s[8 * x : 8 * x + 8, :] = second[x]
    for x, change in enumerate(flow(second, edge1)):
        chg_s[8 * x : 8 * x + 8, :] = change
        field_o[x] = second[x] + change

    for t in range(LINES):
        samp[t : t + 1, :] = v1_s[pl.ds(aline[t], 1), :]
    row8 = iota((8, SUB), 0)

    def windows(tile):
        start = jnp.zeros((8, SUB), jnp.int32)
        for i in range(8):
            start = jnp.where(row8 == i, az[(tile % 2) * 8 + i], start)
        block, shift = start // SUB, start % SUB
        quarter = [samp[8 * tile : 8 * tile + 8, SUB * q : SUB * (q + 1)] for q in range(4)]
        lo = jnp.where(block == 0, quarter[0], jnp.where(block == 1, quarter[1], jnp.where(block == 2, quarter[2], quarter[3])))
        hi = jnp.where(block == 0, quarter[1], jnp.where(block == 1, quarter[2], quarter[3]))
        at = iota((8, SUB), 1) + shift
        index = at % SUB
        return jnp.where(at < SUB, take_lanes(lo, index), take_lanes(hi, index))

    inputs = jnp.concatenate([windows(0), windows(1)], axis=0)
    spectrum = nt(tab_v[0:32, :], inputs, HIGHEST)
    cos_w, sin_w = tab_v[32:48, :], tab_v[48:64, :]
    row16 = iota((16, SUB), 0)
    for t in range(LINES):
        one = slice(SUB * t, SUB * (t + 1))
        ur, ui = spectrum[0:16, t : t + 1], spectrum[16:32, t : t + 1]
        waves = jnp.concatenate([ur * cos_w - ui * sin_w, -(ui * cos_w + ur * sin_w)], axis=0)
        high, low = parts(waves)
        right[0:32, one] = high
        right[80:112, one] = low
        right[160:192, one] = high
        rest = jnp.where(row16 == 0, inputs[t : t + 1, :], jnp.where(row16 == 1, 1.0, 0.0))
        high, low = parts(rest)
        right[64:80, one] = high
        right[144:160, one] = low
        right[224:240, one] = high

    for t in range(LINES):
        samp[LINES + t : LINES + t + 1, :] = chg_s[pl.ds(aline[t], 1), :]
    targets = jnp.concatenate([windows(2), windows(3)], axis=0)

    scale = 1.0 / (TOTAL * SUB)
    proj_grad = jnp.zeros((WIDTH, SUB), F32)
    for pair in range(LINES // 2):
        cols = slice(2 * SUB * pair, 2 * SUB * (pair + 1))
        pre = nn(left3, right[:, cols])
        square = pre * pre
        bend = jnp.tanh(GELU_C * (pre + 0.044715 * (square * pre)))
        half_up = 0.5 * (1.0 + bend)
        hidden = pre * half_up
        slope = half_up + 0.5 * pre * (1.0 - bend * bend) * (GELU_C * (1.0 + 3.0 * 0.044715 * square))
        guess = jnp.sum(hidden * proj, axis=0, keepdims=True)
        target = jnp.concatenate([targets[2 * pair : 2 * pair + 1, :], targets[2 * pair + 1 : 2 * pair + 2, :]], axis=1)
        miss = guess - target
        diff_s[2 * pair : 2 * pair + 1, :] = miss[:, 0:SUB]
        diff_s[2 * pair + 1 : 2 * pair + 2, :] = miss[:, SUB:]
        dq = (2.0 * scale) * miss
        high, low = parts(slope * proj * dq)
        dp_s[0:64, cols] = high
        dp_s[64:128, cols] = low
        back = hidden * dq
        proj_grad = proj_grad + back[:, 0:SUB] + back[:, SUB:]
    grads = nt(dp_s[...], right[0:160, :])
    grads = grads[0:64, 0:KEEP] + grads[0:64, KEEP:] + grads[64:128, 0:KEEP]

    diff = diff_s[...]
    err = jnp.sum(diff * diff, axis=1, keepdims=True)
    eye16 = iota((LINES, LINES), 0) == iota((LINES, LINES), 1)
    err_row = jnp.sum(jnp.where(eye16, err, 0.0), axis=0, keepdims=True)
    named = iota((NS, LINES), 0) == asg_v[...]
    loss = jnp.sum(jnp.where(named, err_row, 0.0), axis=1, keepdims=True) / (LINES * SUB)

    keep = iota((WIDTH, KEEP), 1)
    grads = jnp.where(keep == LANE_PROJ, jnp.sum(proj_grad, axis=1, keepdims=True), grads)
    grads = jnp.where(keep == LANE_LOSS + g, loss, grads)
    payload = jnp.concatenate([grads, jnp.zeros((WIDTH, SUB - KEEP), F32)], axis=1)
    for h in range(2):
        for p in range(NXY):
            pay[h, p] = payload[32 * h + 2 * p : 32 * h + 2 * p + 2, :]

    send(pay.at[1 - c], crs, 4, partner).start()

    pl.semaphore_wait(know.at[1], 2)
    pl.semaphore_wait(know.at[2], 3)
    mom_load.wait()
    for i in Z_ORDER:
        send(mz.at[z], mz.at[z], 2, z_peer(i)).start()

    send(pay.at[1 - c], crs, 4, partner).wait_recv()
    half_s[...] = pay[c] + crs[...]

    for i in XY_ORDER:
        p, device = xy_peer(i)
        send(half_s.at[p], rsb.at[xy], 6, device).start()
    rsb[xy] = half_s[xy]
    arrived(rsb, NXY - 1, 6)
    zrb[z] = jnp.sum(rsb[...], axis=0)

    for i in Z_ORDER:
        send(zrb.at[z], zrb.at[z], 7, z_peer(i)).start()

    arrived(mz, NZ - 1, 2)
    turned = jnp.concatenate([mz[i] for i in range(NZ)], axis=0).T
    gath[c, xy] = jnp.concatenate([turned[0:32, :], turned[32:64, :]], axis=1)
    for i in XY_ORDER:
        send(gath.at[c, xy], gath.at[c, xy], 3, xy_peer(i)[1]).start()

    arrived(zrb, NZ - 1, 7)
    agb[c, xy] = jnp.sum(zrb[...], axis=0)

    for i in XY_ORDER:
        send(agb.at[c, xy], agb.at[c, xy], 8, xy_peer(i)[1]).start()

    arrived(gath.at[c], NXY - 1, 3)
    send(gath.at[c], gath.at[c], 5, partner).start()
    arrived(agb.at[c], NXY - 1, 8)
    send(agb.at[c], agb.at[c], 9, partner).start()

    send(gath.at[1 - c], gath.at[1 - c], 5, partner).wait_recv()
    lane32 = iota((32, SUB), 1)
    for j in range(16):
        for v in range(2):
            index = v * 64 + ((j % 2) * 8 + lane32 // 16) * 4 + lane32 % 4
            four = [take_lanes(gath[k % 2, (j // 2) * 2 + k // 2], index) for k in range(4)]
            moved = jnp.where(
                (lane32 // 8) % 2 == 0,
                jnp.where((lane32 // 4) % 2 == 0, four[0], four[1]),
                jnp.where((lane32 // 4) % 2 == 0, four[2], four[3]),
            )
            at = (slice(32 * v, 32 * v + 32), slice(SUB * j, SUB * (j + 1)))
            base_s[at] = spec_v[at] - (learn_rate * decay_rate) * moved

    send(agb.at[1 - c], agb.at[1 - c], 9, partner).wait_recv()
    total = jnp.concatenate([agb[h, p] for h in range(2) for p in range(NXY)], axis=0)

    lane = iota((WIDTH, SUB), 1)
    gain_back = jnp.zeros((WIDTH, SUB), F32)
    bias_back = jnp.zeros((WIDTH, SUB), F32)
    for j in range(16):
        cols = slice(SUB * j, SUB * (j + 1))
        index = jnp.where(lane < 64, 2 * j, 2 * j + 1)
        by_gain = take_lanes(total, index + LANE_P)
        by_bias = take_lanes(total, index + LANE_Q)
        grad = gain_lanes * by_gain + bias_lanes * by_bias
        grad_s[:, cols] = grad
        spec_o[:, cols] = base_s[:, cols] - learn_rate * grad
        w = spec_v[:, cols]
        gain_back = gain_back + by_gain * w
        bias_back = bias_back + by_bias * w

    dm1, dm0 = total[:, LANE_M1 : LANE_M1 + 1], total[:, LANE_M0 : LANE_M0 + 1]

    def to_column(back, dm):
        both = jnp.sum(back, axis=0, keepdims=True)
        both = both[:, 0:WIDTH] + both[:, WIDTH:] + jnp.sum(mixing * dm, axis=0, keepdims=True)
        return jnp.sum(jnp.where(eye, both, 0.0), axis=1, keepdims=True)

    dense_o[:, 0:64] = mixing - dense_rate * (gain_row * dm1 + bias_row * dm0)
    dense_o[:, 64:65] = dv[:, 64:65] - dense_rate * to_column(gain_back, dm1)
    dense_o[:, 65:66] = dv[:, 65:66] - dense_rate * to_column(bias_back, dm0)
    dense_o[:, 66:67] = layer_bias - dense_rate * dm0
    dense_o[:, 67:68] = proj - dense_rate * total[:, LANE_PROJ : LANE_PROJ + 1]

    mine = grad_s[:, pl.ds(pl.multiple_of((d // 32) * SUB, SUB), SUB)]
    mine = pltpu.roll(mine, lax.rem(SUB - lax.rem(d, 32) * 4, SUB), axis=1)
    mom_o[...] = decay_rate * mz[z] + mine.T[0:4, :]

    own = jnp.logical_and(iota((NS, SUB), 0) == s, lane == LANE_LOSS + g)
    own = jnp.sum(jnp.where(own, total, 0.0), axis=1, keepdims=True)
    loss_o[...] = jnp.sum(own, axis=0, keepdims=True)

    send(side_snd, side_rcv, 0, partner).wait_send()
    send(corn_snd, corn_rcv, 1, partner).wait_send()
    sent(mz, NZ - 1, 2)
    sent(gath.at[c], NXY - 1, 3)
    send(pay.at[1 - c], crs, 4, partner).wait_send()
    send(gath.at[c], gath.at[c], 5, partner).wait_send()
    sent(half_s, NXY - 1, 6)
    sent(zrb, NZ - 1, 7)
    sent(agb.at[c], NXY - 1, 8)
    send(agb.at[c], agb.at[c], 9, partner).wait_send()


def write(*refs):
    sources, results, sems = refs[:5], refs[5:10], refs[10]
    copies = [pltpu.make_async_copy(a, b, sems.at[i]) for i, (a, b) in enumerate(zip(sources, results))]
    for copy in copies:
        copy.start()
    for copy in copies:
        copy.wait()


def local(velocity, rate, forcing, anchor_line, anchor_z, assign, spectral, dense, momentum):
    smem = pl.BlockSpec(memory_space=pltpu.SMEM)
    hbm = pl.BlockSpec(memory_space=pltpu.HBM)
    whole = pl.BlockSpec(memory_space=pltpu.VMEM)
    vmem = pltpu.VMEM
    shapes = (
        jax.ShapeDtypeStruct((8, 8, 512), F32),
        jax.ShapeDtypeStruct((1, 1), F32),
        jax.ShapeDtypeStruct((WIDTH, 2048), F32),
        jax.ShapeDtypeStruct((WIDTH, 68), F32),
        jax.ShapeDtypeStruct((4, WIDTH), F32),
    )

    def pin(x):
        return pltpu.with_memory_space_constraint(x, pltpu.HBM)

    velocity, rate, forcing, momentum = pin(velocity), pin(rate), pin(forcing), pin(momentum)
    anchor_line, anchor_z = pin(anchor_line), pin(anchor_z)
    results = pl.pallas_call(
        kernel,
        out_shape=shapes,
        in_specs=[hbm, hbm, hbm, smem, smem, hbm, hbm, hbm, hbm, hbm],
        out_specs=(whole,) * 5,
        scratch_shapes=[
            vmem((8, 8, 512), F32),
            vmem((8, 8, 512), F32),
            vmem((8, 8, 512), F32),
            vmem((1, LINES), jnp.int32),
            vmem((WIDTH, 2048), F32),
            vmem((WIDTH, 68), F32),
            vmem((96, SUB), F32),
            vmem((4, 3, 8, 512), F32),
            vmem((4, 3, 8, 512), F32),
            vmem((4, 1, 512), F32),
            vmem((4, 1, 512), F32),
            vmem((64, 512), F32),
            vmem((64, 512), F32),
            vmem((2 * LINES, 512), F32),
            vmem((LINES, SUB), F32),
            vmem((3 * KEEP, 2048), BF16),
            vmem((2 * WIDTH, 2048), BF16),
            vmem((NZ, 4, WIDTH), F32),
            vmem((2, NXY, 32, SUB), F32),
            vmem((WIDTH, 2048), F32),
            vmem((WIDTH, 2048), F32),
            vmem((2, NXY, 2, SUB), F32),
            vmem((NXY, 2, SUB), F32),
            vmem((NXY, 2, SUB), F32),
            vmem((NXY, 2, SUB), F32),
            vmem((NZ, 2, SUB), F32),
            vmem((2, NXY, 2, SUB), F32),
            pltpu.SemaphoreType.DMA((8,)),
            pltpu.SemaphoreType.DMA((10,)),
            pltpu.SemaphoreType.DMA((10,)),
            pltpu.SemaphoreType.REGULAR((3,)),
        ],
        compiler_params=pltpu.CompilerParams(
            collective_id=0, has_side_effects=True, vmem_limit_bytes=32 * 1024 * 1024
        ),
    )(velocity, rate, forcing, anchor_line, anchor_z, pin(assign.T), pin(spectral.T), pin(dense.T), momentum, pin(jnp.asarray(tables())))
    field, loss, spec, dens, mom = pl.pallas_call(
        write,
        out_shape=shapes,
        in_specs=[pl.BlockSpec(memory_space=pl.ANY)] * 5,
        out_specs=(hbm,) * 5,
        scratch_shapes=[pltpu.SemaphoreType.DMA((5,))],
        compiler_params=pltpu.CompilerParams(vmem_limit_bytes=1024 * 1024),
    )(*results)
    return (field, loss, spec.T, dens.T, mom)


def solution(mesh):
    placed = (
        P("grp", "slab", None),
        P("grp", "slab", None),
        P("grp", "slab", None),
        P(("grp", "slab")),
        P(("grp", "slab")),
        P(("grp", "slab"), None),
        P(),
        P(),
        P(("grp", "slab"), None),
    )
    return jax.shard_map(
        local,
        mesh=mesh,
        in_specs=placed,
        out_specs=(P("grp", "slab", None), P("grp", "slab"), P(), P(), P(("grp", "slab"), None)),
        check_vma=False,
    )
```

```python
import jax
import jax.numpy as jnp
import numpy as np
from jax import lax
from jax.experimental import pallas as pl
from jax.experimental.pallas import tpu as pltpu
from jax.sharding import PartitionSpec as P

SUB = 128
MODES = 16
WIDTH = 64
LINES = 16
NG = 8
NS = 64
NZ = 16
NXY = 16
TOTAL = 8192

decay_rate = 0.9
learn_rate = 0.5
dense_rate = 3.0

MESH = pl.DeviceIdType.MESH
F32 = jnp.float32
BF16 = jnp.bfloat16
HIGHEST = lax.Precision.HIGHEST
GELU_C = float(np.sqrt(2.0 / np.pi))

Z_ORDER = (8, 7, 9, 6, 10, 5, 11, 4, 12, 3, 13, 2, 14, 1, 15)
Z_NEAR = (3, 13, 2, 14, 1, 15)
XY_ORDER = tuple(
    sorted(
        ((a, b, c) for a in range(2) for b in range(4) for c in range(2) if a + b + c),
        key=lambda i: -(min(i[1], 4 - i[1]) + (2 * i[2] if not i[0] else 1)),
    )
)
PLANE_ORDER = tuple(i + (other,) for i in XY_ORDER for other in (1, 0)) + ((0, 0, 0, 1),)
PLANE_FAR = 14
XY_ROW = ((1, 0, 0), (0, 0, 1), (1, 0, 1))
XY_COLUMN = ((0, 1, 0), (0, 2, 0), (0, 3, 0))

LANE_P = 0
LANE_Q = 32
LANE_M1 = 64
LANE_M0 = 65
LANE_PROJ = 66
LANE_LOSS = 72
KEEP = 80


def tables():
    s = np.arange(SUB)[None, :]
    k = np.arange(MODES)[:, None]
    angle = (k * s % SUB) * (2.0 * np.pi / SUB)
    cos, sin = np.cos(angle), np.sin(angle)
    weight = np.where(k == 0, 1.0, 2.0) / SUB
    er, ei = cos.sum(1, keepdims=True), -sin.sum(1, keepdims=True)
    a0 = weight * (er * cos - ei * sin)
    b0 = -weight * (ei * cos + er * sin)
    return np.concatenate([cos, -sin, weight * cos, weight * sin, a0, b0]).astype(np.float32)


def nt(a, b, precision=None):
    return lax.dot_general(a, b, (((1,), (1,)), ((), ())), precision=precision, preferred_element_type=F32)


def nn(a, b):
    return lax.dot_general(a, b, (((1,), (0,)), ((), ())), preferred_element_type=F32)


def parts(x):
    high = x.astype(BF16)
    return high, (x - high.astype(F32)).astype(BF16)


def iota(shape, dim):
    return lax.broadcasted_iota(jnp.int32, shape, dim)


def take_lanes(x, index):
    return jnp.take_along_axis(x, index, axis=1, mode="promise_in_bounds")


def stencil(mid, others, rate, forc):
    beside = others[0] + others[1] + others[2] + others[3]
    beside = beside + pltpu.roll(mid, 1, axis=1) + pltpu.roll(mid, mid.shape[1] - 1, axis=1)
    return rate * (beside - 6.0 * mid) + forc


def kernel(
    vel, rate, forc, aline_h, az_h, assign, spec, dense, mom, tab,
    field_o, loss_o, spec_o, dense_o, mom_o,
    vel_v, rate_v, forc_v, asg_v, spec_v, dense_v, tab_v,
    side_snd, side_rcv, corn_snd, corn_rcv,
    v1_s, chg_s, samp, diff_s, right, dp_s,
    mz, gath, base_s, grad_s,
    pay, rsb, zrb, agb, aline, az,
    ld, ssem, rsem, know,
):
    g = lax.axis_index("grp")
    s = lax.axis_index("slab")
    z = s // 4
    xc = lax.rem(s, 4)
    xh = xc // 2
    c = lax.rem(xc, 2)
    xy = g * 2 + xh
    d = g * NS + s

    barrier = pltpu.get_barrier_semaphore()

    def greet(device):
        pl.semaphore_signal(barrier, inc=1, device_id=device, device_id_type=MESH)

    xl, y = g // 4, lax.rem(g, 4)

    def z_peer(i):
        return (g, lax.rem(z + i, NZ) * 4 + xc)

    def xy_peer(i):
        flip_l, step, flip_h = i
        gg = (xl + flip_l - 2 * flip_l * xl) * 4 + lax.rem(y + step, 4)
        hh = xh + flip_h - 2 * flip_h * xh
        return gg * 2 + hh, (gg, z * 4 + hh * 2 + c)

    me = c * NXY + xy

    def plane_peer(i):
        p, (gg, ss) = xy_peer(i[:3])
        cc = c + i[3] - 2 * i[3] * c
        return cc * NXY + p, (gg, ss + cc - c)

    up_g, dn_g = lax.rem(g + 1, NG), lax.rem(g + NG - 1, NG)
    up_s, dn_s = lax.rem(s + 1, NS), lax.rem(s + NS - 1, NS)
    sides = [(up_g, s), (dn_g, s), (g, up_s), (g, dn_s)]
    corners = [(up_g, up_s), (up_g, dn_s), (dn_g, up_s), (dn_g, dn_s)]
    partner = (g, s + 1 - 2 * c)

    near = corners + [z_peer(i) for i in Z_NEAR] + [xy_peer(i)[1] for i in XY_ROW + XY_COLUMN] + sides + [partner]

    def load(src, dst, n):
        copy = pltpu.make_async_copy(src, dst, ld.at[n])
        copy.start()
        return copy

    flow_loads = [load(vel, vel_v, 0), load(rate, rate_v, 2), load(forc, forc_v, 3)]
    for device in near:
        greet(device)
    mom_load = load(mom, mz.at[z], 1)
    other_loads = [load(spec, spec_v, 4), load(dense, dense_v, 5), load(tab, tab_v, 6), load(assign, asg_v, 7)]
    other_loads += [load(aline_h, aline, 8), load(az_h, az, 9)]

    def send(src, dst, n, device):
        return pltpu.make_async_remote_copy(
            src_ref=src, dst_ref=dst, send_sem=ssem.at[n], recv_sem=rsem.at[n], device_id=device, device_id_type=MESH
        )

    def arrived(buf, count, n):
        send(buf.at[pl.ds(0, count)], buf.at[pl.ds(0, count)], n, partner).wait_recv()

    def sent(buf, count, n):
        send(buf.at[pl.ds(0, count)], buf.at[pl.ds(0, count)], n, partner).wait_send()

    def tell(n, device):
        pl.semaphore_signal(know.at[n], inc=1, device_id=device, device_id_type=MESH)

    row = iota((8, 512), 0)

    def shifted(plane, before, after):
        lo = jnp.where(row == 0, before, pltpu.roll(plane, 1, axis=0))
        hi = jnp.where(row == 7, after, pltpu.roll(plane, 7, axis=0))
        return lo + hi

    def along(plane):
        return pltpu.roll(plane, 1, axis=1) + pltpu.roll(plane, 511, axis=1)

    for copy in flow_loads:
        copy.wait()
    for n, (a, b) in enumerate([(7, 6), (0, 1), (7, 6), (0, 1)]):
        pick = (lambda ref, i: ref[i]) if n < 2 else (lambda ref, i: ref[:, i, :])
        mid, far, r, f = pick(vel_v, a), pick(vel_v, b), pick(rate_v, a), pick(forc_v, a)
        side_snd[n, 0] = mid
        side_snd[n, 1] = mid + (r * (far + shifted(mid, 0.0, 0.0) + along(mid) - 6.0 * mid) + f)
        side_snd[n, 2] = r
    for n, (a, b) in enumerate([(7, 7), (7, 0), (0, 7), (0, 0)]):
        corn_snd[n] = vel_v[a, b : b + 1, :]
    pl.semaphore_wait(barrier, len(near))
    for n in range(4):
        send(side_snd.at[n], side_rcv.at[n], 0, sides[n]).start()
    for n in range(4):
        send(corn_snd.at[n], corn_rcv.at[n], 1, corners[n]).start()

    for i in (3, NZ - 3):
        tell(0, z_peer(i))
    for i in XY_COLUMN:
        tell(2, xy_peer(i)[1])

    for copy in other_loads:
        copy.wait()
    dv = dense_v[...]
    mixing = dv[:, 0:WIDTH]
    eye = iota((WIDTH, WIDTH), 0) == iota((WIDTH, WIDTH), 1)
    gain_row = jnp.sum(jnp.where(eye, dv[:, 64:65], 0.0), axis=0, keepdims=True)
    bias_row = jnp.sum(jnp.where(eye, dv[:, 65:66], 0.0), axis=0, keepdims=True)
    gain_lanes = jnp.concatenate([gain_row, gain_row], axis=1)
    bias_lanes = jnp.concatenate([bias_row, bias_row], axis=1)
    layer_bias = dv[:, 66:67]
    proj = dv[:, 67:68]
    m1 = jnp.sum(mixing * gain_row, axis=1, keepdims=True)
    m0 = jnp.sum(mixing * bias_row, axis=1, keepdims=True) + layer_bias
    weights = spec_v[...]
    segment = jnp.where(iota((32, 2048), 1) // WIDTH == iota((32, 2048), 0), 1.0, 0.0).astype(BF16)
    gain_high, gain_low = parts(weights * jnp.concatenate([gain_lanes] * 16, axis=1))
    bias_high, bias_low = parts(weights * jnp.concatenate([bias_lanes] * 16, axis=1))
    seen = nt(jnp.concatenate([gain_high, gain_low, bias_high, bias_low], axis=0), segment)
    lane16 = iota((WIDTH, 16), 1)
    left = jnp.concatenate(
        [
            seen[0:64] + seen[64:128],
            seen[128:192] + seen[192:256],
            jnp.where(lane16 == 0, m1, jnp.where(lane16 == 1, m0, 0.0)),
        ],
        axis=1,
    )
    left_high, left_low = parts(left)
    left3 = jnp.concatenate([left_high, left_high, left_low], axis=1)
    for row0, part in zip((32, 112, 192), [parts(tab_v[64:96, :])[i] for i in (0, 1, 0)]):
        for t in range(LINES):
            right[row0 : row0 + 32, SUB * t : SUB * (t + 1)] = part

    pl.semaphore_wait(know.at[2], 3)
    tell(3, partner)
    pl.semaphore_wait(know.at[0], 2)
    for i in (2, NZ - 2):
        tell(1, z_peer(i))

    send(side_snd, side_rcv, 0, partner).wait_recv()
    send(corn_snd, corn_rcv, 1, partner).wait_recv()
    has = [g > 0, g < NG - 1, s > 0, s < NS - 1]
    corner = [
        jnp.where(jnp.logical_and(has[a], has[b]), corn_rcv[n], 0.0)
        for n, (a, b) in enumerate([(0, 2), (0, 3), (1, 2), (1, 3)])
    ]
    edge0, edge1 = [], []
    for n, (a, lo, hi) in enumerate([(0, 0, 1), (7, 2, 3), (0, 0, 2), (7, 1, 3)]):
        mid, part, r = [jnp.where(has[n], side_rcv[n, i], 0.0) for i in range(3)]
        own = vel_v[a] if n < 2 else vel_v[:, a, :]
        ends = jnp.where(row == 0, corner[lo], jnp.where(row == 7, corner[hi], 0.0))
        edge0.append(mid)
        edge1.append(part + r * (own + ends))

    def flow(cells, edge):
        changes = []
        for x in range(8):
            mid = cells[x]
            below = edge[0] if x == 0 else cells[x - 1]
            above = edge[1] if x == 7 else cells[x + 1]
            beside = above + below + shifted(mid, edge[2][x : x + 1, :], edge[3][x : x + 1, :]) + along(mid)
            changes.append(rate_v[x] * (beside - 6.0 * mid) + forc_v[x])
        return changes

    first = [vel_v[x] for x in range(8)]
    second = [mid + change for mid, change in zip(first, flow(first, edge0))]
    for x in range(8):
        v1_s[8 * x : 8 * x + 8, :] = second[x]
    for x, change in enumerate(flow(second, edge1)):
        chg_s[8 * x : 8 * x + 8, :] = change
        field_o[x] = second[x] + change

    for t in range(LINES):
        samp[t : t + 1, :] = v1_s[pl.ds(aline[t], 1), :]
    row8 = iota((8, SUB), 0)

    def windows(tile):
        start = jnp.zeros((8, SUB), jnp.int32)
        for i in range(8):
            start = jnp.where(row8 == i, az[(tile % 2) * 8 + i], start)
        block, shift = start // SUB, start % SUB
        quarter = [samp[8 * tile : 8 * tile + 8, SUB * q : SUB * (q + 1)] for q in range(4)]
        lo = jnp.where(block == 0, quarter[0], jnp.where(block == 1, quarter[1], jnp.where(block == 2, quarter[2], quarter[3])))
        hi = jnp.where(block == 0, quarter[1], jnp.where(block == 1, quarter[2], quarter[3]))
        at = iota((8, SUB), 1) + shift
        index = at % SUB
        return jnp.where(at < SUB, take_lanes(lo, index), take_lanes(hi, index))

    inputs = jnp.concatenate([windows(0), windows(1)], axis=0)
    spectrum = nt(tab_v[0:32, :], inputs, HIGHEST)
    cos_w, sin_w = tab_v[32:48, :], tab_v[48:64, :]
    row16 = iota((16, SUB), 0)
    for t in range(LINES):
        one = slice(SUB * t, SUB * (t + 1))
        ur, ui = spectrum[0:16, t : t + 1], spectrum[16:32, t : t + 1]
        waves = jnp.concatenate([ur * cos_w - ui * sin_w, -(ui * cos_w + ur * sin_w)], axis=0)
        high, low = parts(waves)
        right[0:32, one] = high
        right[80:112, one] = low
        right[160:192, one] = high
        rest = jnp.where(row16 == 0, inputs[t : t + 1, :], jnp.where(row16 == 1, 1.0, 0.0))
        high, low = parts(rest)
        right[64:80, one] = high
        right[144:160, one] = low
        right[224:240, one] = high

    for t in range(LINES):
        samp[LINES + t : LINES + t + 1, :] = chg_s[pl.ds(aline[t], 1), :]
    targets = jnp.concatenate([windows(2), windows(3)], axis=0)

    scale = 1.0 / (TOTAL * SUB)
    proj_grad = jnp.zeros((WIDTH, SUB), F32)
    for pair in range(LINES // 2):
        cols = slice(2 * SUB * pair, 2 * SUB * (pair + 1))
        pre = nn(left3, right[:, cols])
        square = pre * pre
        bend = jnp.tanh(GELU_C * (pre + 0.044715 * (square * pre)))
        half_up = 0.5 * (1.0 + bend)
        hidden = pre * half_up
        slope = half_up + 0.5 * pre * (1.0 - bend * bend) * (GELU_C * (1.0 + 3.0 * 0.044715 * square))
        guess = jnp.sum(hidden * proj, axis=0, keepdims=True)
        target = jnp.concatenate([targets[2 * pair : 2 * pair + 1, :], targets[2 * pair + 1 : 2 * pair + 2, :]], axis=1)
        miss = guess - target
        diff_s[2 * pair : 2 * pair + 1, :] = miss[:, 0:SUB]
        diff_s[2 * pair + 1 : 2 * pair + 2, :] = miss[:, SUB:]
        dq = (2.0 * scale) * miss
        high, low = parts(slope * proj * dq)
        dp_s[0:64, cols] = high
        dp_s[64:128, cols] = low
        back = hidden * dq
        proj_grad = proj_grad + back[:, 0:SUB] + back[:, SUB:]
    grads = nt(dp_s[...], right[0:160, :])
    grads = grads[0:64, 0:KEEP] + grads[0:64, KEEP:] + grads[64:128, 0:KEEP]

    diff = diff_s[...]
    err = jnp.sum(diff * diff, axis=1, keepdims=True)
    eye16 = iota((LINES, LINES), 0) == iota((LINES, LINES), 1)
    err_row = jnp.sum(jnp.where(eye16, err, 0.0), axis=0, keepdims=True)
    named = iota((NS, LINES), 0) == asg_v[...]
    loss = jnp.sum(jnp.where(named, err_row, 0.0), axis=1, keepdims=True) / (LINES * SUB)

    keep = iota((WIDTH, KEEP), 1)
    grads = jnp.where(keep == LANE_PROJ, jnp.sum(proj_grad, axis=1, keepdims=True), grads)
    grads = jnp.where(keep == LANE_LOSS + g, loss, grads)
    payload = jnp.concatenate([grads, jnp.zeros((WIDTH, SUB - KEEP), F32)], axis=1)
    for p in range(2 * NXY):
        pay[p] = payload[2 * p : 2 * p + 2, :]

    def scatter(order):
        for i in order:
            p, device = plane_peer(i)
            send(pay.at[p], rsb.at[me], 6, device).start()

    pl.semaphore_wait(know.at[3], 1)
    scatter(PLANE_ORDER[:PLANE_FAR])

    pl.semaphore_wait(know.at[1], 2)
    mom_load.wait()
    for i in Z_ORDER:
        send(mz.at[z], mz.at[z], 2, z_peer(i)).start()

    scatter(PLANE_ORDER[PLANE_FAR:])
    rsb[me] = pay[me]
    arrived(rsb, 2 * NXY - 1, 6)
    zrb[z] = jnp.sum(rsb[...], axis=0)

    for i in Z_ORDER:
        send(zrb.at[z], zrb.at[z], 7, z_peer(i)).start()

    arrived(mz, NZ - 1, 2)
    turned = jnp.concatenate([mz[i] for i in range(NZ)], axis=0).T
    gath[c, xy] = jnp.concatenate([turned[0:32, :], turned[32:64, :]], axis=1)
    for i in XY_ORDER:
        send(gath.at[c, xy], gath.at[c, xy], 3, xy_peer(i)[1]).start()

    arrived(zrb, NZ - 1, 7)
    agb[me] = jnp.sum(zrb[...], axis=0)
    for i in PLANE_ORDER:
        send(agb.at[me], agb.at[me], 4, plane_peer(i)[1]).start()

    arrived(gath.at[c], NXY - 1, 3)
    send(gath.at[c], gath.at[c], 5, partner).start()
    lane32 = iota((32, SUB), 1)

    def unpack(share, before):
        for j in range(16):
            for v in range(2):
                index = v * 64 + ((j % 2) * 8 + lane32 // 16) * 4 + lane32 % 4
                two = [take_lanes(gath[share, (j // 2) * 2 + h], index) for h in range(2)]
                moved = jnp.where((lane32 // 8) % 2 == 0, two[0], two[1])
                moved = jnp.where((lane32 // 4) % 2 == share, moved, 0.0)
                at = (slice(32 * v, 32 * v + 32), slice(SUB * j, SUB * (j + 1)))
                base_s[at] = before[at] - (learn_rate * decay_rate) * moved

    unpack(c, spec_v)
    send(gath.at[1 - c], gath.at[1 - c], 5, partner).wait_recv()
    unpack(1 - c, base_s)
    arrived(agb, 2 * NXY - 1, 4)
    total = jnp.concatenate([agb[p] for p in range(2 * NXY)], axis=0)

    lane = iota((WIDTH, SUB), 1)
    gain_back = jnp.zeros((WIDTH, SUB), F32)
    bias_back = jnp.zeros((WIDTH, SUB), F32)
    for j in range(16):
        cols = slice(SUB * j, SUB * (j + 1))
        index = jnp.where(lane < 64, 2 * j, 2 * j + 1)
        by_gain = take_lanes(total, index + LANE_P)
        by_bias = take_lanes(total, index + LANE_Q)
        grad = gain_lanes * by_gain + bias_lanes * by_bias
        grad_s[:, cols] = grad
        spec_o[:, cols] = base_s[:, cols] - learn_rate * grad
        w = spec_v[:, cols]
        gain_back = gain_back + by_gain * w
        bias_back = bias_back + by_bias * w

    dm1, dm0 = total[:, LANE_M1 : LANE_M1 + 1], total[:, LANE_M0 : LANE_M0 + 1]

    def to_column(back, dm):
        both = jnp.sum(back, axis=0, keepdims=True)
        both = both[:, 0:WIDTH] + both[:, WIDTH:] + jnp.sum(mixing * dm, axis=0, keepdims=True)
        return jnp.sum(jnp.where(eye, both, 0.0), axis=1, keepdims=True)

    dense_o[:, 0:64] = mixing - dense_rate * (gain_row * dm1 + bias_row * dm0)
    dense_o[:, 64:65] = dv[:, 64:65] - dense_rate * to_column(gain_back, dm1)
    dense_o[:, 65:66] = dv[:, 65:66] - dense_rate * to_column(bias_back, dm0)
    dense_o[:, 66:67] = layer_bias - dense_rate * dm0
    dense_o[:, 67:68] = proj - dense_rate * total[:, LANE_PROJ : LANE_PROJ + 1]

    mine = grad_s[:, pl.ds(pl.multiple_of((d // 32) * SUB, SUB), SUB)]
    mine = pltpu.roll(mine, lax.rem(SUB - lax.rem(d, 32) * 4, SUB), axis=1)
    mom_o[...] = decay_rate * mz[z] + mine.T[0:4, :]

    own = jnp.logical_and(iota((NS, SUB), 0) == s, lane == LANE_LOSS + g)
    own = jnp.sum(jnp.where(own, total, 0.0), axis=1, keepdims=True)
    loss_o[...] = jnp.sum(own, axis=0, keepdims=True)

    send(side_snd, side_rcv, 0, partner).wait_send()
    send(corn_snd, corn_rcv, 1, partner).wait_send()
    sent(mz, NZ - 1, 2)
    sent(gath.at[c], NXY - 1, 3)
    send(gath.at[c], gath.at[c], 5, partner).wait_send()
    sent(pay, 2 * NXY - 1, 6)
    sent(zrb, NZ - 1, 7)
    sent(agb, 2 * NXY - 1, 4)


def write(*refs):
    sources, results, sems = refs[:5], refs[5:10], refs[10]
    copies = [pltpu.make_async_copy(a, b, sems.at[i]) for i, (a, b) in enumerate(zip(sources, results))]
    for copy in copies:
        copy.start()
    for copy in copies:
        copy.wait()


def local(velocity, rate, forcing, anchor_line, anchor_z, assign, spectral, dense, momentum):
    hbm = pl.BlockSpec(memory_space=pltpu.HBM)
    whole = pl.BlockSpec(memory_space=pltpu.VMEM)
    vmem = pltpu.VMEM
    shapes = (
        jax.ShapeDtypeStruct((8, 8, 512), F32),
        jax.ShapeDtypeStruct((1, 1), F32),
        jax.ShapeDtypeStruct((WIDTH, 2048), F32),
        jax.ShapeDtypeStruct((WIDTH, 68), F32),
        jax.ShapeDtypeStruct((4, WIDTH), F32),
    )

    def pin(x):
        return pltpu.with_memory_space_constraint(x, pltpu.HBM)

    velocity, rate, forcing, momentum = pin(velocity), pin(rate), pin(forcing), pin(momentum)
    anchor_line, anchor_z = pin(anchor_line), pin(anchor_z)
    results = pl.pallas_call(
        kernel,
        out_shape=shapes,
        in_specs=[hbm] * 10,
        out_specs=(whole,) * 5,
        scratch_shapes=[
            vmem((8, 8, 512), F32),
            vmem((8, 8, 512), F32),
            vmem((8, 8, 512), F32),
            vmem((1, LINES), jnp.int32),
            vmem((WIDTH, 2048), F32),
            vmem((WIDTH, 68), F32),
            vmem((96, SUB), F32),
            vmem((4, 3, 8, 512), F32),
            vmem((4, 3, 8, 512), F32),
            vmem((4, 1, 512), F32),
            vmem((4, 1, 512), F32),
            vmem((64, 512), F32),
            vmem((64, 512), F32),
            vmem((2 * LINES, 512), F32),
            vmem((LINES, SUB), F32),
            vmem((3 * KEEP, 2048), BF16),
            vmem((2 * WIDTH, 2048), BF16),
            vmem((NZ, 4, WIDTH), F32),
            vmem((2, NXY, 32, SUB), F32),
            vmem((WIDTH, 2048), F32),
            vmem((WIDTH, 2048), F32),
            vmem((2 * NXY, 2, SUB), F32),
            vmem((2 * NXY, 2, SUB), F32),
            vmem((NZ, 2, SUB), F32),
            vmem((2 * NXY, 2, SUB), F32),
            pltpu.SMEM((LINES,), jnp.int32),
            pltpu.SMEM((LINES,), jnp.int32),
            pltpu.SemaphoreType.DMA((10,)),
            pltpu.SemaphoreType.DMA((8,)),
            pltpu.SemaphoreType.DMA((8,)),
            pltpu.SemaphoreType.REGULAR((4,)),
        ],
        compiler_params=pltpu.CompilerParams(
            collective_id=0, has_side_effects=True, vmem_limit_bytes=32 * 1024 * 1024
        ),
    )(velocity, rate, forcing, anchor_line, anchor_z, pin(assign.T), pin(spectral.T), pin(dense.T), momentum, pin(jnp.asarray(tables())))
    field, loss, spec, dens, mom = pl.pallas_call(
        write,
        out_shape=shapes,
        in_specs=[pl.BlockSpec(memory_space=pl.ANY)] * 5,
        out_specs=(hbm,) * 5,
        scratch_shapes=[pltpu.SemaphoreType.DMA((5,))],
        compiler_params=pltpu.CompilerParams(vmem_limit_bytes=1024 * 1024),
    )(*results)
    return (field, loss, spec.T, dens.T, mom)


def solution(mesh):
    placed = (
        P("grp", "slab", None),
        P("grp", "slab", None),
        P("grp", "slab", None),
        P(("grp", "slab")),
        P(("grp", "slab")),
        P(("grp", "slab"), None),
        P(),
        P(),
        P(("grp", "slab"), None),
    )
    return jax.shard_map(
        local,
        mesh=mesh,
        in_specs=placed,
        out_specs=(P("grp", "slab", None), P("grp", "slab"), P(), P(), P(("grp", "slab"), None)),
        check_vma=False,
    )
```

```python
import jax
import jax.numpy as jnp
import numpy as np
from jax import lax
from jax.experimental import pallas as pl
from jax.experimental.pallas import tpu as pltpu
from jax.sharding import PartitionSpec as P

SUB = 128
MODES = 16
WIDTH = 64
LINES = 16
NG = 8
NS = 64
NZ = 16
NXY = 16
TOTAL = 8192

decay_rate = 0.9
learn_rate = 0.5
dense_rate = 3.0

MESH = pl.DeviceIdType.MESH
F32 = jnp.float32
BF16 = jnp.bfloat16
HIGHEST = lax.Precision.HIGHEST
GELU_C = float(np.sqrt(2.0 / np.pi))

Z_ORDER = (8, 7, 9, 6, 10, 5, 11, 4, 12, 3, 13, 2, 14, 1, 15)
Z_NEAR = (4, 12, 3, 13, 2, 14, 1, 15)
XY_ORDER = tuple(
    sorted(
        ((a, b, c) for a in range(2) for b in range(4) for c in range(2) if a + b + c),
        key=lambda i: -(min(i[1], 4 - i[1]) + (2 * i[2] if not i[0] else 1)),
    )
)
PLANE_ORDER = tuple(i + (other,) for i in XY_ORDER for other in (1, 0)) + ((0, 0, 0, 1),)
XY_ROW = ((1, 0, 0), (0, 0, 1), (1, 0, 1))
XY_COLUMN = ((0, 1, 0), (0, 2, 0), (0, 3, 0))

LANE_P = 0
LANE_Q = 32
LANE_M1 = 64
LANE_M0 = 65
LANE_PROJ = 66
LANE_LOSS = 72
KEEP = 80


def tables():
    s = np.arange(SUB)[None, :]
    k = np.arange(MODES)[:, None]
    angle = (k * s % SUB) * (2.0 * np.pi / SUB)
    cos, sin = np.cos(angle), np.sin(angle)
    weight = np.where(k == 0, 1.0, 2.0) / SUB
    er, ei = cos.sum(1, keepdims=True), -sin.sum(1, keepdims=True)
    a0 = weight * (er * cos - ei * sin)
    b0 = -weight * (ei * cos + er * sin)
    return np.concatenate([cos, -sin, weight * cos, weight * sin, a0, b0]).astype(np.float32)


def nt(a, b, precision=None):
    return lax.dot_general(a, b, (((1,), (1,)), ((), ())), precision=precision, preferred_element_type=F32)


def nn(a, b):
    return lax.dot_general(a, b, (((1,), (0,)), ((), ())), preferred_element_type=F32)


def parts(x):
    high = x.astype(BF16)
    return high, (x - high.astype(F32)).astype(BF16)


def iota(shape, dim):
    return lax.broadcasted_iota(jnp.int32, shape, dim)


def take_lanes(x, index):
    return jnp.take_along_axis(x, index, axis=1, mode="promise_in_bounds")


def stencil(mid, others, rate, forc):
    beside = others[0] + others[1] + others[2] + others[3]
    beside = beside + pltpu.roll(mid, 1, axis=1) + pltpu.roll(mid, mid.shape[1] - 1, axis=1)
    return rate * (beside - 6.0 * mid) + forc


def kernel(
    vel, rate, forc, aline_h, az_h, assign, spec, dense, mom, tab,
    field_o, loss_o, spec_o, dense_o, mom_o,
    vel_v, rate_v, forc_v, asg_v, spec_v, dense_v, tab_v,
    side_snd, side_rcv, corn_snd, corn_rcv,
    v1_s, chg_s, samp, diff_s, right, dp_s,
    mz, gath, base_s, grad_s,
    pay, rsb, zrb, agb, aline, az,
    ld, ssem, rsem, know,
):
    g = lax.axis_index("grp")
    s = lax.axis_index("slab")
    z = s // 4
    xc = lax.rem(s, 4)
    xh = xc // 2
    c = lax.rem(xc, 2)
    xy = g * 2 + xh
    d = g * NS + s

    barrier = pltpu.get_barrier_semaphore()

    def greet(device):
        pl.semaphore_signal(barrier, inc=1, device_id=device, device_id_type=MESH)

    xl, y = g // 4, lax.rem(g, 4)

    def z_peer(i):
        return (g, lax.rem(z + i, NZ) * 4 + xc)

    def xy_peer(i):
        flip_l, step, flip_h = i
        gg = (xl + flip_l - 2 * flip_l * xl) * 4 + lax.rem(y + step, 4)
        hh = xh + flip_h - 2 * flip_h * xh
        return gg * 2 + hh, (gg, z * 4 + hh * 2 + c)

    me = c * NXY + xy

    def plane_peer(i):
        p, (gg, ss) = xy_peer(i[:3])
        cc = c + i[3] - 2 * i[3] * c
        return cc * NXY + p, (gg, ss + cc - c)

    up_g, dn_g = lax.rem(g + 1, NG), lax.rem(g + NG - 1, NG)
    up_s, dn_s = lax.rem(s + 1, NS), lax.rem(s + NS - 1, NS)
    sides = [(up_g, s), (dn_g, s), (g, up_s), (g, dn_s)]
    corners = [(up_g, up_s), (up_g, dn_s), (dn_g, up_s), (dn_g, dn_s)]
    partner = (g, s + 1 - 2 * c)

    near = corners + [z_peer(i) for i in Z_NEAR] + [xy_peer(i)[1] for i in XY_ROW + XY_COLUMN] + sides + [partner]

    def load(src, dst, n):
        copy = pltpu.make_async_copy(src, dst, ld.at[n])
        copy.start()
        return copy

    flow_loads = [load(vel, vel_v, 0), load(rate, rate_v, 2), load(forc, forc_v, 3)]
    for device in near:
        greet(device)
    mom_load = load(mom, mz.at[z], 1)
    other_loads = [load(spec, spec_v, 4), load(dense, dense_v, 5), load(tab, tab_v, 6), load(assign, asg_v, 7)]
    other_loads += [load(aline_h, aline, 8), load(az_h, az, 9)]

    def send(src, dst, n, device):
        return pltpu.make_async_remote_copy(
            src_ref=src, dst_ref=dst, send_sem=ssem.at[n], recv_sem=rsem.at[n], device_id=device, device_id_type=MESH
        )

    def arrived(buf, count, n):
        send(buf.at[pl.ds(0, count)], buf.at[pl.ds(0, count)], n, partner).wait_recv()

    def sent(buf, count, n):
        send(buf.at[pl.ds(0, count)], buf.at[pl.ds(0, count)], n, partner).wait_send()

    def tell(n, device):
        pl.semaphore_signal(know.at[n], inc=1, device_id=device, device_id_type=MESH)

    row = iota((8, 512), 0)

    def shifted(plane, before, after):
        lo = jnp.where(row == 0, before, pltpu.roll(plane, 1, axis=0))
        hi = jnp.where(row == 7, after, pltpu.roll(plane, 7, axis=0))
        return lo + hi

    def along(plane):
        return pltpu.roll(plane, 1, axis=1) + pltpu.roll(plane, 511, axis=1)

    for copy in flow_loads:
        copy.wait()
    for n, (a, b) in enumerate([(7, 6), (0, 1), (7, 6), (0, 1)]):
        pick = (lambda ref, i: ref[i]) if n < 2 else (lambda ref, i: ref[:, i, :])
        mid, far, r, f = pick(vel_v, a), pick(vel_v, b), pick(rate_v, a), pick(forc_v, a)
        side_snd[n, 0] = mid
        side_snd[n, 1] = mid + (r * (far + shifted(mid, 0.0, 0.0) + along(mid) - 6.0 * mid) + f)
        side_snd[n, 2] = r
    for n, (a, b) in enumerate([(7, 7), (7, 0), (0, 7), (0, 0)]):
        corn_snd[n] = vel_v[a, b : b + 1, :]
    pl.semaphore_wait(barrier, len(near))
    for n in range(4):
        send(side_snd.at[n], side_rcv.at[n], 0, sides[n]).start()
    for n in range(4):
        send(corn_snd.at[n], corn_rcv.at[n], 1, corners[n]).start()

    for i in (4, NZ - 4):
        tell(0, z_peer(i))
    for i in XY_COLUMN:
        tell(1, xy_peer(i)[1])

    for copy in other_loads:
        copy.wait()
    dv = dense_v[...]
    mixing = dv[:, 0:WIDTH]
    eye = iota((WIDTH, WIDTH), 0) == iota((WIDTH, WIDTH), 1)
    gain_row = jnp.sum(jnp.where(eye, dv[:, 64:65], 0.0), axis=0, keepdims=True)
    bias_row = jnp.sum(jnp.where(eye, dv[:, 65:66], 0.0), axis=0, keepdims=True)
    gain_lanes = jnp.concatenate([gain_row, gain_row], axis=1)
    bias_lanes = jnp.concatenate([bias_row, bias_row], axis=1)
    layer_bias = dv[:, 66:67]
    proj = dv[:, 67:68]
    m1 = jnp.sum(mixing * gain_row, axis=1, keepdims=True)
    m0 = jnp.sum(mixing * bias_row, axis=1, keepdims=True) + layer_bias
    weights = spec_v[...]
    segment = jnp.where(iota((32, 2048), 1) // WIDTH == iota((32, 2048), 0), 1.0, 0.0).astype(BF16)
    gain_high, gain_low = parts(weights * jnp.concatenate([gain_lanes] * 16, axis=1))
    bias_high, bias_low = parts(weights * jnp.concatenate([bias_lanes] * 16, axis=1))
    seen = nt(jnp.concatenate([gain_high, gain_low, bias_high, bias_low], axis=0), segment)
    lane16 = iota((WIDTH, 16), 1)
    left = jnp.concatenate(
        [
            seen[0:64] + seen[64:128],
            seen[128:192] + seen[192:256],
            jnp.where(lane16 == 0, m1, jnp.where(lane16 == 1, m0, 0.0)),
        ],
        axis=1,
    )
    left_high, left_low = parts(left)
    left3 = jnp.concatenate([left_high, left_high, left_low], axis=1)
    for row0, part in zip((32, 112, 192), [parts(tab_v[64:96, :])[i] for i in (0, 1, 0)]):
        for t in range(LINES):
            right[row0 : row0 + 32, SUB * t : SUB * (t + 1)] = part

    pl.semaphore_wait(know.at[1], 3)
    tell(2, partner)
    pl.semaphore_wait(know.at[0], 2)
    mom_load.wait()
    for i in Z_ORDER:
        send(mz.at[z], mz.at[z], 2, z_peer(i)).start()

    send(side_snd, side_rcv, 0, partner).wait_recv()
    has = [g > 0, g < NG - 1, s > 0, s < NS - 1]
    edge0 = [jnp.where(has[n], side_rcv[n, 0], 0.0) for n in range(4)]

    def flow(cells, edge):
        changes = []
        for x in range(8):
            mid = cells[x]
            below = edge[0] if x == 0 else cells[x - 1]
            above = edge[1] if x == 7 else cells[x + 1]
            beside = above + below + shifted(mid, edge[2][x : x + 1, :], edge[3][x : x + 1, :]) + along(mid)
            changes.append(rate_v[x] * (beside - 6.0 * mid) + forc_v[x])
        return changes

    first = [vel_v[x] for x in range(8)]
    second = [mid + change for mid, change in zip(first, flow(first, edge0))]
    for x in range(8):
        v1_s[8 * x : 8 * x + 8, :] = second[x]
    for t in range(LINES):
        samp[t : t + 1, :] = v1_s[pl.ds(aline[t], 1), :]
    row8 = iota((8, SUB), 0)

    def windows(tile):
        start = jnp.zeros((8, SUB), jnp.int32)
        for i in range(8):
            start = jnp.where(row8 == i, az[(tile % 2) * 8 + i], start)
        block, shift = start // SUB, start % SUB
        quarter = [samp[8 * tile : 8 * tile + 8, SUB * q : SUB * (q + 1)] for q in range(4)]
        lo = jnp.where(block == 0, quarter[0], jnp.where(block == 1, quarter[1], jnp.where(block == 2, quarter[2], quarter[3])))
        hi = jnp.where(block == 0, quarter[1], jnp.where(block == 1, quarter[2], quarter[3]))
        at = iota((8, SUB), 1) + shift
        index = at % SUB
        return jnp.where(at < SUB, take_lanes(lo, index), take_lanes(hi, index))

    inputs = jnp.concatenate([windows(0), windows(1)], axis=0)
    spectrum = nt(tab_v[0:32, :], inputs, HIGHEST)
    cos_w, sin_w = tab_v[32:48, :], tab_v[48:64, :]
    row16 = iota((16, SUB), 0)
    for t in range(LINES):
        one = slice(SUB * t, SUB * (t + 1))
        ur, ui = spectrum[0:16, t : t + 1], spectrum[16:32, t : t + 1]
        waves = jnp.concatenate([ur * cos_w - ui * sin_w, -(ui * cos_w + ur * sin_w)], axis=0)
        high, low = parts(waves)
        right[0:32, one] = high
        right[80:112, one] = low
        right[160:192, one] = high
        rest = jnp.where(row16 == 0, inputs[t : t + 1, :], jnp.where(row16 == 1, 1.0, 0.0))
        high, low = parts(rest)
        right[64:80, one] = high
        right[144:160, one] = low
        right[224:240, one] = high

    send(corn_snd, corn_rcv, 1, partner).wait_recv()
    corner = [
        jnp.where(jnp.logical_and(has[a], has[b]), corn_rcv[n], 0.0)
        for n, (a, b) in enumerate([(0, 2), (0, 3), (1, 2), (1, 3)])
    ]
    edge1 = []
    for n, (a, lo, hi) in enumerate([(0, 0, 1), (7, 2, 3), (0, 0, 2), (7, 1, 3)]):
        part, r = [jnp.where(has[n], side_rcv[n, i], 0.0) for i in (1, 2)]
        own = vel_v[a] if n < 2 else vel_v[:, a, :]
        ends = jnp.where(row == 0, corner[lo], jnp.where(row == 7, corner[hi], 0.0))
        edge1.append(part + r * (own + ends))

    for x, change in enumerate(flow(second, edge1)):
        chg_s[8 * x : 8 * x + 8, :] = change
        field_o[x] = second[x] + change
    for t in range(LINES):
        samp[LINES + t : LINES + t + 1, :] = chg_s[pl.ds(aline[t], 1), :]
    targets = jnp.concatenate([windows(2), windows(3)], axis=0)

    scale = 1.0 / (TOTAL * SUB)
    proj_grad = jnp.zeros((WIDTH, SUB), F32)
    for pair in range(LINES // 2):
        cols = slice(2 * SUB * pair, 2 * SUB * (pair + 1))
        pre = nn(left3, right[:, cols])
        square = pre * pre
        bend = jnp.tanh(GELU_C * (pre + 0.044715 * (square * pre)))
        half_up = 0.5 * (1.0 + bend)
        hidden = pre * half_up
        slope = half_up + 0.5 * pre * (1.0 - bend * bend) * (GELU_C * (1.0 + 3.0 * 0.044715 * square))
        guess = jnp.sum(hidden * proj, axis=0, keepdims=True)
        target = jnp.concatenate([targets[2 * pair : 2 * pair + 1, :], targets[2 * pair + 1 : 2 * pair + 2, :]], axis=1)
        miss = guess - target
        diff_s[2 * pair : 2 * pair + 1, :] = miss[:, 0:SUB]
        diff_s[2 * pair + 1 : 2 * pair + 2, :] = miss[:, SUB:]
        dq = (2.0 * scale) * miss
        high, low = parts(slope * proj * dq)
        dp_s[0:64, cols] = high
        dp_s[64:128, cols] = low
        back = hidden * dq
        proj_grad = proj_grad + back[:, 0:SUB] + back[:, SUB:]
    grads = nt(dp_s[...], right[0:160, :])
    grads = grads[0:64, 0:KEEP] + grads[0:64, KEEP:] + grads[64:128, 0:KEEP]

    diff = diff_s[...]
    err = jnp.sum(diff * diff, axis=1, keepdims=True)
    eye16 = iota((LINES, LINES), 0) == iota((LINES, LINES), 1)
    err_row = jnp.sum(jnp.where(eye16, err, 0.0), axis=0, keepdims=True)
    named = iota((NS, LINES), 0) == asg_v[...]
    loss = jnp.sum(jnp.where(named, err_row, 0.0), axis=1, keepdims=True) / (LINES * SUB)

    keep = iota((WIDTH, KEEP), 1)
    grads = jnp.where(keep == LANE_PROJ, jnp.sum(proj_grad, axis=1, keepdims=True), grads)
    grads = jnp.where(keep == LANE_LOSS + g, loss, grads)
    payload = jnp.concatenate([grads, jnp.zeros((WIDTH, SUB - KEEP), F32)], axis=1)
    for p in range(2 * NXY):
        pay[p] = payload[2 * p : 2 * p + 2, :]

    def scatter(order):
        for i in order:
            p, device = plane_peer(i)
            send(pay.at[p], rsb.at[me], 6, device).start()

    pl.semaphore_wait(know.at[2], 1)
    scatter(PLANE_ORDER)
    rsb[me] = pay[me]
    arrived(rsb, 2 * NXY - 1, 6)
    zrb[z] = jnp.sum(rsb[...], axis=0)

    for i in Z_ORDER:
        send(zrb.at[z], zrb.at[z], 7, z_peer(i)).start()

    arrived(mz, NZ - 1, 2)
    turned = jnp.concatenate([mz[i] for i in range(NZ)], axis=0).T
    gath[c, xy] = jnp.concatenate([turned[0:32, :], turned[32:64, :]], axis=1)
    for i in XY_ORDER:
        send(gath.at[c, xy], gath.at[c, xy], 3, xy_peer(i)[1]).start()

    arrived(zrb, NZ - 1, 7)
    agb[me] = jnp.sum(zrb[...], axis=0)
    for i in PLANE_ORDER:
        send(agb.at[me], agb.at[me], 4, plane_peer(i)[1]).start()

    arrived(gath.at[c], NXY - 1, 3)
    send(gath.at[c], gath.at[c], 5, partner).start()
    lane32 = iota((32, SUB), 1)

    def unpack(share, before):
        for j in range(16):
            for v in range(2):
                index = v * 64 + ((j % 2) * 8 + lane32 // 16) * 4 + lane32 % 4
                two = [take_lanes(gath[share, (j // 2) * 2 + h], index) for h in range(2)]
                moved = jnp.where((lane32 // 8) % 2 == 0, two[0], two[1])
                moved = jnp.where((lane32 // 4) % 2 == share, moved, 0.0)
                at = (slice(32 * v, 32 * v + 32), slice(SUB * j, SUB * (j + 1)))
                base_s[at] = before[at] - (learn_rate * decay_rate) * moved

    unpack(c, spec_v)
    send(gath.at[1 - c], gath.at[1 - c], 5, partner).wait_recv()
    unpack(1 - c, base_s)
    arrived(agb, 2 * NXY - 1, 4)
    total = jnp.concatenate([agb[p] for p in range(2 * NXY)], axis=0)

    lane = iota((WIDTH, SUB), 1)
    gain_back = jnp.zeros((WIDTH, SUB), F32)
    bias_back = jnp.zeros((WIDTH, SUB), F32)
    for j in range(16):
        cols = slice(SUB * j, SUB * (j + 1))
        index = jnp.where(lane < 64, 2 * j, 2 * j + 1)
        by_gain = take_lanes(total, index + LANE_P)
        by_bias = take_lanes(total, index + LANE_Q)
        grad = gain_lanes * by_gain + bias_lanes * by_bias
        grad_s[:, cols] = grad
        spec_o[:, cols] = base_s[:, cols] - learn_rate * grad
        w = spec_v[:, cols]
        gain_back = gain_back + by_gain * w
        bias_back = bias_back + by_bias * w

    dm1, dm0 = total[:, LANE_M1 : LANE_M1 + 1], total[:, LANE_M0 : LANE_M0 + 1]

    def to_column(back, dm):
        both = jnp.sum(back, axis=0, keepdims=True)
        both = both[:, 0:WIDTH] + both[:, WIDTH:] + jnp.sum(mixing * dm, axis=0, keepdims=True)
        return jnp.sum(jnp.where(eye, both, 0.0), axis=1, keepdims=True)

    dense_o[:, 0:64] = mixing - dense_rate * (gain_row * dm1 + bias_row * dm0)
    dense_o[:, 64:65] = dv[:, 64:65] - dense_rate * to_column(gain_back, dm1)
    dense_o[:, 65:66] = dv[:, 65:66] - dense_rate * to_column(bias_back, dm0)
    dense_o[:, 66:67] = layer_bias - dense_rate * dm0
    dense_o[:, 67:68] = proj - dense_rate * total[:, LANE_PROJ : LANE_PROJ + 1]

    mine = grad_s[:, pl.ds(pl.multiple_of((d // 32) * SUB, SUB), SUB)]
    mine = pltpu.roll(mine, lax.rem(SUB - lax.rem(d, 32) * 4, SUB), axis=1)
    mom_o[...] = decay_rate * mz[z] + mine.T[0:4, :]

    own = jnp.logical_and(iota((NS, SUB), 0) == s, lane == LANE_LOSS + g)
    own = jnp.sum(jnp.where(own, total, 0.0), axis=1, keepdims=True)
    loss_o[...] = jnp.sum(own, axis=0, keepdims=True)

    send(side_snd, side_rcv, 0, partner).wait_send()
    send(corn_snd, corn_rcv, 1, partner).wait_send()
    sent(mz, NZ - 1, 2)
    sent(gath.at[c], NXY - 1, 3)
    send(gath.at[c], gath.at[c], 5, partner).wait_send()
    sent(pay, 2 * NXY - 1, 6)
    sent(zrb, NZ - 1, 7)
    sent(agb, 2 * NXY - 1, 4)


def write(*refs):
    sources, results, sems = refs[:5], refs[5:10], refs[10]
    pairs = [(sources[2].at[pl.ds(16 * i, 16)], results[2].at[pl.ds(16 * i, 16)]) for i in range(4)]
    pairs += [(sources[0].at[pl.ds(4 * i, 4)], results[0].at[pl.ds(4 * i, 4)]) for i in range(2)]
    pairs += [(sources[i], results[i]) for i in (1, 3, 4)]
    copies = [pltpu.make_async_copy(a, b, sems.at[i]) for i, (a, b) in enumerate(pairs)]
    for copy in copies:
        copy.start()
    for copy in copies:
        copy.wait()


def local(velocity, rate, forcing, anchor_line, anchor_z, assign, spectral, dense, momentum):
    hbm = pl.BlockSpec(memory_space=pltpu.HBM)
    whole = pl.BlockSpec(memory_space=pltpu.VMEM)
    vmem = pltpu.VMEM
    shapes = (
        jax.ShapeDtypeStruct((8, 8, 512), F32),
        jax.ShapeDtypeStruct((1, 1), F32),
        jax.ShapeDtypeStruct((WIDTH, 2048), F32),
        jax.ShapeDtypeStruct((WIDTH, 68), F32),
        jax.ShapeDtypeStruct((4, WIDTH), F32),
    )

    def pin(x):
        return pltpu.with_memory_space_constraint(x, pltpu.HBM)

    velocity, rate, forcing, momentum = pin(velocity), pin(rate), pin(forcing), pin(momentum)
    anchor_line, anchor_z = pin(anchor_line), pin(anchor_z)
    results = pl.pallas_call(
        kernel,
        out_shape=shapes,
        in_specs=[hbm] * 10,
        out_specs=(whole,) * 5,
        scratch_shapes=[
            vmem((8, 8, 512), F32),
            vmem((8, 8, 512), F32),
            vmem((8, 8, 512), F32),
            vmem((1, LINES), jnp.int32),
            vmem((WIDTH, 2048), F32),
            vmem((WIDTH, 68), F32),
            vmem((96, SUB), F32),
            vmem((4, 3, 8, 512), F32),
            vmem((4, 3, 8, 512), F32),
            vmem((4, 1, 512), F32),
            vmem((4, 1, 512), F32),
            vmem((64, 512), F32),
            vmem((64, 512), F32),
            vmem((2 * LINES, 512), F32),
            vmem((LINES, SUB), F32),
            vmem((3 * KEEP, 2048), BF16),
            vmem((2 * WIDTH, 2048), BF16),
            vmem((NZ, 4, WIDTH), F32),
            vmem((2, NXY, 32, SUB), F32),
            vmem((WIDTH, 2048), F32),
            vmem((WIDTH, 2048), F32),
            vmem((2 * NXY, 2, SUB), F32),
            vmem((2 * NXY, 2, SUB), F32),
            vmem((NZ, 2, SUB), F32),
            vmem((2 * NXY, 2, SUB), F32),
            pltpu.SMEM((LINES,), jnp.int32),
            pltpu.SMEM((LINES,), jnp.int32),
            pltpu.SemaphoreType.DMA((10,)),
            pltpu.SemaphoreType.DMA((8,)),
            pltpu.SemaphoreType.DMA((8,)),
            pltpu.SemaphoreType.REGULAR((3,)),
        ],
        compiler_params=pltpu.CompilerParams(
            collective_id=0, has_side_effects=True, vmem_limit_bytes=32 * 1024 * 1024
        ),
    )(velocity, rate, forcing, anchor_line, anchor_z, pin(assign.T), pin(spectral.T), pin(dense.T), momentum, pin(jnp.asarray(tables())))
    field, loss, spec, dens, mom = pl.pallas_call(
        write,
        out_shape=shapes,
        in_specs=[pl.BlockSpec(memory_space=pl.ANY)] * 5,
        out_specs=(hbm,) * 5,
        scratch_shapes=[pltpu.SemaphoreType.DMA((9,))],
        compiler_params=pltpu.CompilerParams(vmem_limit_bytes=1024 * 1024),
    )(*results)
    return (field, loss, spec.T, dens.T, mom)


def solution(mesh):
    placed = (
        P("grp", "slab", None),
        P("grp", "slab", None),
        P("grp", "slab", None),
        P(("grp", "slab")),
        P(("grp", "slab")),
        P(("grp", "slab"), None),
        P(),
        P(),
        P(("grp", "slab"), None),
    )
    return jax.shard_map(
        local,
        mesh=mesh,
        in_specs=placed,
        out_specs=(P("grp", "slab", None), P("grp", "slab"), P(), P(), P(("grp", "slab"), None)),
        check_vma=False,
    )
```

```python
import jax
import jax.numpy as jnp
import numpy as np
from jax import lax
from jax.experimental import pallas as pl
from jax.experimental.pallas import tpu as pltpu
from jax.sharding import PartitionSpec as P

SUB = 128
MODES = 16
WIDTH = 64
LINES = 16
NG = 8
NS = 64
NZ = 16
NXY = 16
TOTAL = 8192

decay_rate = 0.9
learn_rate = 0.5
dense_rate = 3.0

MESH = pl.DeviceIdType.MESH
F32 = jnp.float32
BF16 = jnp.bfloat16
HIGHEST = lax.Precision.HIGHEST
GELU_C = float(np.sqrt(2.0 / np.pi))

Z_ORDER = (8, 7, 9, 6, 10, 5, 11, 4, 12, 3, 13, 2, 14, 1, 15)
Z_NEAR = (4, 12, 3, 13, 2, 14, 1, 15)
XY_ORDER = tuple(
    sorted(
        ((a, b, c) for a in range(2) for b in range(4) for c in range(2) if a + b + c),
        key=lambda i: -(min(i[1], 4 - i[1]) + (2 * i[2] if not i[0] else 1)),
    )
)
PLANE_ORDER = tuple(i + (other,) for i in XY_ORDER for other in (1, 0)) + ((0, 0, 0, 1),)
RING_ORDER = tuple(i for i in PLANE_ORDER if i[1] == 0)
XY_ROW = ((1, 0, 0), (0, 0, 1), (1, 0, 1))
XY_COLUMN = ((0, 1, 0), (0, 2, 0), (0, 3, 0))

LANE_P = 0
LANE_Q = 32
LANE_M1 = 64
LANE_M0 = 65
LANE_PROJ = 66
LANE_LOSS = 72
KEEP = 80


def tables():
    s = np.arange(SUB)[None, :]
    k = np.arange(MODES)[:, None]
    angle = (k * s % SUB) * (2.0 * np.pi / SUB)
    cos, sin = np.cos(angle), np.sin(angle)
    weight = np.where(k == 0, 1.0, 2.0) / SUB
    er, ei = cos.sum(1, keepdims=True), -sin.sum(1, keepdims=True)
    a0 = weight * (er * cos - ei * sin)
    b0 = -weight * (ei * cos + er * sin)
    return np.concatenate([cos, -sin, weight * cos, weight * sin, a0, b0]).astype(np.float32)


def nt(a, b, precision=None):
    return lax.dot_general(a, b, (((1,), (1,)), ((), ())), precision=precision, preferred_element_type=F32)


def nn(a, b):
    return lax.dot_general(a, b, (((1,), (0,)), ((), ())), preferred_element_type=F32)


def parts(x):
    high = x.astype(BF16)
    return high, (x - high.astype(F32)).astype(BF16)


def iota(shape, dim):
    return lax.broadcasted_iota(jnp.int32, shape, dim)


def take_lanes(x, index):
    return jnp.take_along_axis(x, index, axis=1, mode="promise_in_bounds")


def stencil(mid, others, rate, forc):
    beside = others[0] + others[1] + others[2] + others[3]
    beside = beside + pltpu.roll(mid, 1, axis=1) + pltpu.roll(mid, mid.shape[1] - 1, axis=1)
    return rate * (beside - 6.0 * mid) + forc


def kernel(
    vel, rate, forc, aline_h, az_h, assign, spec, dense, mom, tab,
    field_o, loss_o, spec_o, dense_o, mom_o,
    vel_v, rate_v, forc_v, asg_v, spec_v, dense_v, tab_v,
    side_snd, side_rcv, corn_snd, corn_rcv,
    v1_s, chg_s, samp, diff_s, right, dp_s,
    mz, gath, base_s, grad_s,
    pay, rsb, zrb, agb, aline, az,
    ld, ssem, rsem, know,
):
    g = lax.axis_index("grp")
    s = lax.axis_index("slab")
    z = s // 4
    xc = lax.rem(s, 4)
    xh = xc // 2
    c = lax.rem(xc, 2)
    xy = g * 2 + xh
    d = g * NS + s

    barrier = pltpu.get_barrier_semaphore()

    def greet(device):
        pl.semaphore_signal(barrier, inc=1, device_id=device, device_id_type=MESH)

    xl, y = g // 4, lax.rem(g, 4)

    def z_peer(i):
        return (g, lax.rem(z + i, NZ) * 4 + xc)

    def xy_peer(i):
        flip_l, step, flip_h = i
        gg = (xl + flip_l - 2 * flip_l * xl) * 4 + lax.rem(y + step, 4)
        hh = xh + flip_h - 2 * flip_h * xh
        return gg * 2 + hh, (gg, z * 4 + hh * 2 + c)

    me = c * NXY + xy
    piece = (xl * 2 + xh) * 2 + c

    def plane_peer(i):
        p, (gg, ss) = xy_peer(i[:3])
        cc = c + i[3] - 2 * i[3] * c
        return (p // 8 * 2 + lax.rem(p, 2)) * 2 + cc, (gg, ss + cc - c)

    up_g, dn_g = lax.rem(g + 1, NG), lax.rem(g + NG - 1, NG)
    up_s, dn_s = lax.rem(s + 1, NS), lax.rem(s + NS - 1, NS)
    sides = [(up_g, s), (dn_g, s), (g, up_s), (g, dn_s)]
    corners = [(up_g, up_s), (up_g, dn_s), (dn_g, up_s), (dn_g, dn_s)]
    partner = (g, s + 1 - 2 * c)

    near = corners + [z_peer(i) for i in Z_NEAR] + [xy_peer(i)[1] for i in XY_ROW + XY_COLUMN] + sides + [partner]

    def load(src, dst, n):
        copy = pltpu.make_async_copy(src, dst, ld.at[n])
        copy.start()
        return copy

    for device in near:
        greet(device)
    flow_loads = [load(vel, vel_v, 0), load(rate, rate_v, 2), load(forc, forc_v, 3)]
    mom_load = load(mom, mz.at[z], 1)
    other_loads = [load(spec, spec_v, 4), load(dense, dense_v, 5), load(tab, tab_v, 6), load(assign, asg_v, 7)]
    other_loads += [load(aline_h, aline, 8), load(az_h, az, 9)]

    def send(src, dst, n, device):
        return pltpu.make_async_remote_copy(
            src_ref=src, dst_ref=dst, send_sem=ssem.at[n], recv_sem=rsem.at[n], device_id=device, device_id_type=MESH
        )

    def arrived(buf, count, n):
        send(buf.at[pl.ds(0, count)], buf.at[pl.ds(0, count)], n, partner).wait_recv()

    def sent(buf, count, n):
        send(buf.at[pl.ds(0, count)], buf.at[pl.ds(0, count)], n, partner).wait_send()

    def tell(n, device):
        pl.semaphore_signal(know.at[n], inc=1, device_id=device, device_id_type=MESH)

    row = iota((8, 512), 0)

    def shifted(plane, before, after):
        lo = jnp.where(row == 0, before, pltpu.roll(plane, 1, axis=0))
        hi = jnp.where(row == 7, after, pltpu.roll(plane, 7, axis=0))
        return lo + hi

    def along(plane):
        return pltpu.roll(plane, 1, axis=1) + pltpu.roll(plane, 511, axis=1)

    for copy in flow_loads:
        copy.wait()
    for n, (a, b) in enumerate([(7, 6), (0, 1), (7, 6), (0, 1)]):
        pick = (lambda ref, i: ref[i]) if n < 2 else (lambda ref, i: ref[:, i, :])
        mid, far, r, f = pick(vel_v, a), pick(vel_v, b), pick(rate_v, a), pick(forc_v, a)
        side_snd[n, 0] = mid
        side_snd[n, 1] = mid + (r * (far + shifted(mid, 0.0, 0.0) + along(mid) - 6.0 * mid) + f)
        side_snd[n, 2] = r
    for n, (a, b) in enumerate([(7, 7), (7, 0), (0, 7), (0, 0)]):
        corn_snd[n] = vel_v[a, b : b + 1, :]
    pl.semaphore_wait(barrier, len(near))
    for n in range(4):
        send(side_snd.at[n], side_rcv.at[n], 0, sides[n]).start()
    for n in range(4):
        send(corn_snd.at[n], corn_rcv.at[n], 1, corners[n]).start()

    for i in (4, NZ - 4):
        tell(0, z_peer(i))
    for i in XY_COLUMN:
        tell(1, xy_peer(i)[1])

    for copy in other_loads:
        copy.wait()
    dv = dense_v[...]
    mixing = dv[:, 0:WIDTH]
    eye = iota((WIDTH, WIDTH), 0) == iota((WIDTH, WIDTH), 1)
    gain_row = jnp.sum(jnp.where(eye, dv[:, 64:65], 0.0), axis=0, keepdims=True)
    bias_row = jnp.sum(jnp.where(eye, dv[:, 65:66], 0.0), axis=0, keepdims=True)
    gain_lanes = jnp.concatenate([gain_row, gain_row], axis=1)
    bias_lanes = jnp.concatenate([bias_row, bias_row], axis=1)
    layer_bias = dv[:, 66:67]
    proj = dv[:, 67:68]
    m1 = jnp.sum(mixing * gain_row, axis=1, keepdims=True)
    m0 = jnp.sum(mixing * bias_row, axis=1, keepdims=True) + layer_bias
    weights = spec_v[...]
    segment = jnp.where(iota((32, 2048), 1) // WIDTH == iota((32, 2048), 0), 1.0, 0.0).astype(BF16)
    gain_high, gain_low = parts(weights * jnp.concatenate([gain_lanes] * 16, axis=1))
    bias_high, bias_low = parts(weights * jnp.concatenate([bias_lanes] * 16, axis=1))
    seen = nt(jnp.concatenate([gain_high, gain_low, bias_high, bias_low], axis=0), segment)
    lane16 = iota((WIDTH, 16), 1)
    left = jnp.concatenate(
        [
            seen[0:64] + seen[64:128],
            seen[128:192] + seen[192:256],
            jnp.where(lane16 == 0, m1, jnp.where(lane16 == 1, m0, 0.0)),
        ],
        axis=1,
    )
    left_high, left_low = parts(left)
    left3 = jnp.concatenate([left_high, left_high, left_low], axis=1)
    for row0, part in zip((32, 112, 192), [parts(tab_v[64:96, :])[i] for i in (0, 1, 0)]):
        for t in range(LINES):
            right[row0 : row0 + 32, SUB * t : SUB * (t + 1)] = part

    pl.semaphore_wait(know.at[1], 3)
    tell(2, partner)
    pl.semaphore_wait(know.at[0], 2)
    mom_load.wait()
    for i in Z_ORDER:
        send(mz.at[z], mz.at[z], 2, z_peer(i)).start()

    send(side_snd, side_rcv, 0, partner).wait_recv()
    has = [g > 0, g < NG - 1, s > 0, s < NS - 1]
    edge0 = [jnp.where(has[n], side_rcv[n, 0], 0.0) for n in range(4)]

    def flow(cells, edge):
        changes = []
        for x in range(8):
            mid = cells[x]
            below = edge[0] if x == 0 else cells[x - 1]
            above = edge[1] if x == 7 else cells[x + 1]
            beside = above + below + shifted(mid, edge[2][x : x + 1, :], edge[3][x : x + 1, :]) + along(mid)
            changes.append(rate_v[x] * (beside - 6.0 * mid) + forc_v[x])
        return changes

    first = [vel_v[x] for x in range(8)]
    second = [mid + change for mid, change in zip(first, flow(first, edge0))]
    for x in range(8):
        v1_s[8 * x : 8 * x + 8, :] = second[x]
    for t in range(LINES):
        samp[t : t + 1, :] = v1_s[pl.ds(aline[t], 1), :]
    row8 = iota((8, SUB), 0)

    def windows(tile):
        start = jnp.zeros((8, SUB), jnp.int32)
        for i in range(8):
            start = jnp.where(row8 == i, az[(tile % 2) * 8 + i], start)
        block, shift = start // SUB, start % SUB
        quarter = [samp[8 * tile : 8 * tile + 8, SUB * q : SUB * (q + 1)] for q in range(4)]
        lo = jnp.where(block == 0, quarter[0], jnp.where(block == 1, quarter[1], jnp.where(block == 2, quarter[2], quarter[3])))
        hi = jnp.where(block == 0, quarter[1], jnp.where(block == 1, quarter[2], quarter[3]))
        at = iota((8, SUB), 1) + shift
        index = at % SUB
        return jnp.where(at < SUB, take_lanes(lo, index), take_lanes(hi, index))

    inputs = jnp.concatenate([windows(0), windows(1)], axis=0)
    spectrum = nt(tab_v[0:32, :], inputs, HIGHEST)
    cos_w, sin_w = tab_v[32:48, :], tab_v[48:64, :]
    row16 = iota((16, SUB), 0)
    for t in range(LINES):
        one = slice(SUB * t, SUB * (t + 1))
        ur, ui = spectrum[0:16, t : t + 1], spectrum[16:32, t : t + 1]
        waves = jnp.concatenate([ur * cos_w - ui * sin_w, -(ui * cos_w + ur * sin_w)], axis=0)
        high, low = parts(waves)
        right[0:32, one] = high
        right[80:112, one] = low
        right[160:192, one] = high
        rest = jnp.where(row16 == 0, inputs[t : t + 1, :], jnp.where(row16 == 1, 1.0, 0.0))
        high, low = parts(rest)
        right[64:80, one] = high
        right[144:160, one] = low
        right[224:240, one] = high

    send(corn_snd, corn_rcv, 1, partner).wait_recv()
    corner = [
        jnp.where(jnp.logical_and(has[a], has[b]), corn_rcv[n], 0.0)
        for n, (a, b) in enumerate([(0, 2), (0, 3), (1, 2), (1, 3)])
    ]
    edge1 = []
    for n, (a, lo, hi) in enumerate([(0, 0, 1), (7, 2, 3), (0, 0, 2), (7, 1, 3)]):
        part, r = [jnp.where(has[n], side_rcv[n, i], 0.0) for i in (1, 2)]
        own = vel_v[a] if n < 2 else vel_v[:, a, :]
        ends = jnp.where(row == 0, corner[lo], jnp.where(row == 7, corner[hi], 0.0))
        edge1.append(part + r * (own + ends))

    for x, change in enumerate(flow(second, edge1)):
        chg_s[8 * x : 8 * x + 8, :] = change
        field_o[x] = second[x] + change
    for t in range(LINES):
        samp[LINES + t : LINES + t + 1, :] = chg_s[pl.ds(aline[t], 1), :]
    targets = jnp.concatenate([windows(2), windows(3)], axis=0)

    scale = 1.0 / (TOTAL * SUB)
    proj_grad = jnp.zeros((WIDTH, SUB), F32)
    for pair in range(LINES // 2):
        cols = slice(2 * SUB * pair, 2 * SUB * (pair + 1))
        pre = nn(left3, right[:, cols])
        square = pre * pre
        bend = jnp.tanh(GELU_C * (pre + 0.044715 * (square * pre)))
        half_up = 0.5 * (1.0 + bend)
        hidden = pre * half_up
        slope = half_up + 0.5 * pre * (1.0 - bend * bend) * (GELU_C * (1.0 + 3.0 * 0.044715 * square))
        guess = jnp.sum(hidden * proj, axis=0, keepdims=True)
        target = jnp.concatenate([targets[2 * pair : 2 * pair + 1, :], targets[2 * pair + 1 : 2 * pair + 2, :]], axis=1)
        miss = guess - target
        diff_s[2 * pair : 2 * pair + 1, :] = miss[:, 0:SUB]
        diff_s[2 * pair + 1 : 2 * pair + 2, :] = miss[:, SUB:]
        dq = (2.0 * scale) * miss
        high, low = parts(slope * proj * dq)
        dp_s[0:64, cols] = high
        dp_s[64:128, cols] = low
        back = hidden * dq
        proj_grad = proj_grad + back[:, 0:SUB] + back[:, SUB:]
    grads = nt(dp_s[...], right[0:160, :])
    grads = grads[0:64, 0:KEEP] + grads[0:64, KEEP:] + grads[64:128, 0:KEEP]

    diff = diff_s[...]
    err = jnp.sum(diff * diff, axis=1, keepdims=True)
    eye16 = iota((LINES, LINES), 0) == iota((LINES, LINES), 1)
    err_row = jnp.sum(jnp.where(eye16, err, 0.0), axis=0, keepdims=True)
    named = iota((NS, LINES), 0) == asg_v[...]
    loss = jnp.sum(jnp.where(named, err_row, 0.0), axis=1, keepdims=True) / (LINES * SUB)

    keep = iota((WIDTH, KEEP), 1)
    grads = jnp.where(keep == LANE_PROJ, jnp.sum(proj_grad, axis=1, keepdims=True), grads)
    grads = jnp.where(keep == LANE_LOSS + g, loss, grads)
    payload = jnp.concatenate([grads, jnp.zeros((WIDTH, SUB - KEEP), F32)], axis=1)
    for p in range(8):
        pay[p] = payload[8 * p : 8 * p + 8, :]

    def scatter(order):
        for i in order:
            p, device = plane_peer(i)
            send(pay.at[p], rsb.at[me], 6, device).start()

    pl.semaphore_wait(know.at[2], 1)
    scatter(PLANE_ORDER)
    rsb[me] = pay[piece]
    arrived(rsb, 2 * NXY - 1, 6)
    zrb[z] = jnp.sum(rsb[...], axis=0)

    for i in Z_ORDER:
        send(zrb.at[z], zrb.at[z], 7, z_peer(i)).start()

    arrived(mz, NZ - 1, 2)
    turned = jnp.concatenate([mz[i] for i in range(NZ)], axis=0).T
    gath[c, xy] = jnp.concatenate([turned[0:32, :], turned[32:64, :]], axis=1)
    for i in XY_ORDER:
        send(gath.at[c, xy], gath.at[c, xy], 3, xy_peer(i)[1]).start()

    arrived(zrb, NZ - 1, 7)
    agb[piece] = jnp.sum(zrb[...], axis=0)
    for i in RING_ORDER:
        send(agb.at[piece], agb.at[piece], 4, plane_peer(i)[1]).start()

    arrived(gath.at[c], NXY - 1, 3)
    send(gath.at[c], gath.at[c], 5, partner).start()
    lane32 = iota((32, SUB), 1)

    def unpack(share, before):
        for j in range(16):
            for v in range(2):
                index = v * 64 + ((j % 2) * 8 + lane32 // 16) * 4 + lane32 % 4
                two = [take_lanes(gath[share, (j // 2) * 2 + h], index) for h in range(2)]
                moved = jnp.where((lane32 // 8) % 2 == 0, two[0], two[1])
                moved = jnp.where((lane32 // 4) % 2 == share, moved, 0.0)
                at = (slice(32 * v, 32 * v + 32), slice(SUB * j, SUB * (j + 1)))
                base_s[at] = before[at] - (learn_rate * decay_rate) * moved

    unpack(c, spec_v)
    send(gath.at[1 - c], gath.at[1 - c], 5, partner).wait_recv()
    unpack(1 - c, base_s)
    arrived(agb, 7, 4)
    total = agb[...].reshape(WIDTH, SUB)

    lane = iota((WIDTH, SUB), 1)
    gain_back = jnp.zeros((WIDTH, SUB), F32)
    bias_back = jnp.zeros((WIDTH, SUB), F32)
    for j in range(16):
        cols = slice(SUB * j, SUB * (j + 1))
        index = jnp.where(lane < 64, 2 * j, 2 * j + 1)
        by_gain = take_lanes(total, index + LANE_P)
        by_bias = take_lanes(total, index + LANE_Q)
        grad = gain_lanes * by_gain + bias_lanes * by_bias
        grad_s[:, cols] = grad
        spec_o[:, cols] = base_s[:, cols] - learn_rate * grad
        w = spec_v[:, cols]
        gain_back = gain_back + by_gain * w
        bias_back = bias_back + by_bias * w

    dm1, dm0 = total[:, LANE_M1 : LANE_M1 + 1], total[:, LANE_M0 : LANE_M0 + 1]

    def to_column(back, dm):
        both = jnp.sum(back, axis=0, keepdims=True)
        both = both[:, 0:WIDTH] + both[:, WIDTH:] + jnp.sum(mixing * dm, axis=0, keepdims=True)
        return jnp.sum(jnp.where(eye, both, 0.0), axis=1, keepdims=True)

    dense_o[:, 0:64] = mixing - dense_rate * (gain_row * dm1 + bias_row * dm0)
    dense_o[:, 64:65] = dv[:, 64:65] - dense_rate * to_column(gain_back, dm1)
    dense_o[:, 65:66] = dv[:, 65:66] - dense_rate * to_column(bias_back, dm0)
    dense_o[:, 66:67] = layer_bias - dense_rate * dm0
    dense_o[:, 67:68] = proj - dense_rate * total[:, LANE_PROJ : LANE_PROJ + 1]

    mine = grad_s[:, pl.ds(pl.multiple_of((d // 32) * SUB, SUB), SUB)]
    mine = pltpu.roll(mine, lax.rem(SUB - lax.rem(d, 32) * 4, SUB), axis=1)
    mom_o[...] = decay_rate * mz[z] + mine.T[0:4, :]

    own = jnp.logical_and(iota((NS, SUB), 0) == s, lane == LANE_LOSS + g)
    own = jnp.sum(jnp.where(own, total, 0.0), axis=1, keepdims=True)
    loss_o[...] = jnp.sum(own, axis=0, keepdims=True)

    send(side_snd, side_rcv, 0, partner).wait_send()
    send(corn_snd, corn_rcv, 1, partner).wait_send()
    sent(mz, NZ - 1, 2)
    sent(gath.at[c], NXY - 1, 3)
    send(gath.at[c], gath.at[c], 5, partner).wait_send()
    sent(rsb, 2 * NXY - 1, 6)
    sent(zrb, NZ - 1, 7)
    sent(agb, 7, 4)


def write(*refs):
    sources, results, sems = refs[:5], refs[5:10], refs[10]
    pairs = [(sources[2].at[pl.ds(16 * i, 16)], results[2].at[pl.ds(16 * i, 16)]) for i in range(4)]
    pairs += [(sources[0].at[pl.ds(4 * i, 4)], results[0].at[pl.ds(4 * i, 4)]) for i in range(2)]
    pairs += [(sources[i], results[i]) for i in (1, 3, 4)]
    copies = [pltpu.make_async_copy(a, b, sems.at[i]) for i, (a, b) in enumerate(pairs)]
    for copy in copies:
        copy.start()
    for copy in copies:
        copy.wait()


def local(velocity, rate, forcing, anchor_line, anchor_z, assign, spectral, dense, momentum):
    hbm = pl.BlockSpec(memory_space=pltpu.HBM)
    whole = pl.BlockSpec(memory_space=pltpu.VMEM)
    vmem = pltpu.VMEM
    shapes = (
        jax.ShapeDtypeStruct((8, 8, 512), F32),
        jax.ShapeDtypeStruct((1, 1), F32),
        jax.ShapeDtypeStruct((WIDTH, 2048), F32),
        jax.ShapeDtypeStruct((WIDTH, 68), F32),
        jax.ShapeDtypeStruct((4, WIDTH), F32),
    )

    def pin(x):
        return pltpu.with_memory_space_constraint(x, pltpu.HBM)

    velocity, rate, forcing, momentum = pin(velocity), pin(rate), pin(forcing), pin(momentum)
    anchor_line, anchor_z = pin(anchor_line), pin(anchor_z)
    results = pl.pallas_call(
        kernel,
        out_shape=shapes,
        in_specs=[hbm] * 10,
        out_specs=(whole,) * 5,
        scratch_shapes=[
            vmem((8, 8, 512), F32),
            vmem((8, 8, 512), F32),
            vmem((8, 8, 512), F32),
            vmem((1, LINES), jnp.int32),
            vmem((WIDTH, 2048), F32),
            vmem((WIDTH, 68), F32),
            vmem((96, SUB), F32),
            vmem((4, 3, 8, 512), F32),
            vmem((4, 3, 8, 512), F32),
            vmem((4, 1, 512), F32),
            vmem((4, 1, 512), F32),
            vmem((64, 512), F32),
            vmem((64, 512), F32),
            vmem((2 * LINES, 512), F32),
            vmem((LINES, SUB), F32),
            vmem((3 * KEEP, 2048), BF16),
            vmem((2 * WIDTH, 2048), BF16),
            vmem((NZ, 4, WIDTH), F32),
            vmem((2, NXY, 32, SUB), F32),
            vmem((WIDTH, 2048), F32),
            vmem((WIDTH, 2048), F32),
            vmem((8, 8, SUB), F32),
            vmem((2 * NXY, 8, SUB), F32),
            vmem((NZ, 8, SUB), F32),
            vmem((8, 8, SUB), F32),
            pltpu.SMEM((LINES,), jnp.int32),
            pltpu.SMEM((LINES,), jnp.int32),
            pltpu.SemaphoreType.DMA((10,)),
            pltpu.SemaphoreType.DMA((8,)),
            pltpu.SemaphoreType.DMA((8,)),
            pltpu.SemaphoreType.REGULAR((3,)),
        ],
        compiler_params=pltpu.CompilerParams(
            collective_id=0, has_side_effects=True, vmem_limit_bytes=32 * 1024 * 1024
        ),
    )(velocity, rate, forcing, anchor_line, anchor_z, pin(assign.T), pin(spectral.T), pin(dense.T), momentum, pin(jnp.asarray(tables())))
    field, loss, spec, dens, mom = pl.pallas_call(
        write,
        out_shape=shapes,
        in_specs=[pl.BlockSpec(memory_space=pl.ANY)] * 5,
        out_specs=(hbm,) * 5,
        scratch_shapes=[pltpu.SemaphoreType.DMA((9,))],
        compiler_params=pltpu.CompilerParams(vmem_limit_bytes=1024 * 1024),
    )(*results)
    return (field, loss, spec.T, dens.T, mom)


def solution(mesh):
    placed = (
        P("grp", "slab", None),
        P("grp", "slab", None),
        P("grp", "slab", None),
        P(("grp", "slab")),
        P(("grp", "slab")),
        P(("grp", "slab"), None),
        P(),
        P(),
        P(("grp", "slab"), None),
    )
    return jax.shard_map(
        local,
        mesh=mesh,
        in_specs=placed,
        out_specs=(P("grp", "slab", None), P("grp", "slab"), P(), P(), P(("grp", "slab"), None)),
        check_vma=False,
    )
```

```python
import jax
import jax.numpy as jnp
import numpy as np
from jax import lax
from jax.experimental import pallas as pl
from jax.experimental.pallas import tpu as pltpu
from jax.sharding import PartitionSpec as P

SUB = 128
MODES = 16
WIDTH = 64
LINES = 16
NG = 8
NS = 64
NZ = 16
NXY = 16
TOTAL = 8192

decay_rate = 0.9
learn_rate = 0.5
dense_rate = 3.0

MESH = pl.DeviceIdType.MESH
F32 = jnp.float32
BF16 = jnp.bfloat16
GELU_C = float(np.sqrt(2.0 / np.pi))

Z_ORDER = (8, 7, 9, 6, 10, 5, 11, 4, 12, 3, 13, 2, 14, 1, 15)
Z_NEAR = (4, 12, 3, 13, 2, 14, 1, 15)
XY_ORDER = tuple(
    sorted(
        ((a, b, c) for a in range(2) for b in range(4) for c in range(2) if a + b + c),
        key=lambda i: -(min(i[1], 4 - i[1]) + (2 * i[2] if not i[0] else 1)),
    )
)
PLANE_ORDER = tuple(i + (other,) for i in XY_ORDER for other in (1, 0)) + ((0, 0, 0, 1),)
RING_ORDER = tuple(i for i in PLANE_ORDER if i[1] == 0)
XY_ROW = ((1, 0, 0), (0, 0, 1), (1, 0, 1))
XY_COLUMN = ((0, 1, 0), (0, 2, 0), (0, 3, 0))

LANE_P = 0
LANE_Q = 32
LANE_M1 = 64
LANE_M0 = 65
LANE_PROJ = 66
LANE_LOSS = 72
KEEP = 80


def tables():
    s = np.arange(SUB)[None, :]
    k = np.arange(MODES)[:, None]
    angle = (k * s % SUB) * (2.0 * np.pi / SUB)
    cos, sin = np.cos(angle), np.sin(angle)
    weight = np.where(k == 0, 1.0, 2.0) / SUB
    er, ei = cos.sum(1, keepdims=True), -sin.sum(1, keepdims=True)
    a0 = weight * (er * cos - ei * sin)
    b0 = -weight * (ei * cos + er * sin)
    return np.concatenate([cos, -sin, weight * cos, weight * sin, a0, b0]).astype(np.float32)


def nt(a, b):
    return lax.dot_general(a, b, (((1,), (1,)), ((), ())), preferred_element_type=F32)


def nn(a, b):
    return lax.dot_general(a, b, (((1,), (0,)), ((), ())), preferred_element_type=F32)


def parts(x):
    high = x.astype(BF16)
    return high, (x - high.astype(F32)).astype(BF16)


def iota(shape, dim):
    return lax.broadcasted_iota(jnp.int32, shape, dim)


def take_lanes(x, index):
    return jnp.take_along_axis(x, index, axis=1, mode="promise_in_bounds")


def stencil(mid, others, rate, forc):
    beside = others[0] + others[1] + others[2] + others[3]
    beside = beside + pltpu.roll(mid, 1, axis=1) + pltpu.roll(mid, mid.shape[1] - 1, axis=1)
    return rate * (beside - 6.0 * mid) + forc


def kernel(
    vel, rate, forc, aline_h, az_h, assign, spec, dense, mom, tab,
    field_o, loss_o, spec_o, dense_o, mom_o,
    vel_v, rate_v, forc_v, asg_v, spec_v, dense_v, tab_v,
    side_snd, side_rcv, corn_snd, corn_rcv,
    v1_s, chg_s, samp, diff_s, right, dp_s,
    mz, gath, base_s, grad_s,
    pay, rsb, zrb, agb, aline, az,
    ld, ssem, rsem, know,
):
    g = lax.axis_index("grp")
    s = lax.axis_index("slab")
    z = s // 4
    xc = lax.rem(s, 4)
    xh = xc // 2
    c = lax.rem(xc, 2)
    xy = g * 2 + xh
    d = g * NS + s

    barrier = pltpu.get_barrier_semaphore()

    def greet(device):
        pl.semaphore_signal(barrier, inc=1, device_id=device, device_id_type=MESH)

    xl, y = g // 4, lax.rem(g, 4)

    def z_peer(i):
        return (g, lax.rem(z + i, NZ) * 4 + xc)

    def xy_peer(i):
        flip_l, step, flip_h = i
        gg = (xl + flip_l - 2 * flip_l * xl) * 4 + lax.rem(y + step, 4)
        hh = xh + flip_h - 2 * flip_h * xh
        return gg * 2 + hh, (gg, z * 4 + hh * 2 + c)

    me = c * NXY + xy
    piece = (xl * 2 + xh) * 2 + c

    def plane_peer(i):
        p, (gg, ss) = xy_peer(i[:3])
        cc = c + i[3] - 2 * i[3] * c
        return (p // 8 * 2 + lax.rem(p, 2)) * 2 + cc, (gg, ss + cc - c)

    up_g, dn_g = lax.rem(g + 1, NG), lax.rem(g + NG - 1, NG)
    up_s, dn_s = lax.rem(s + 1, NS), lax.rem(s + NS - 1, NS)
    sides = [(up_g, s), (dn_g, s), (g, up_s), (g, dn_s)]
    corners = [(up_g, up_s), (up_g, dn_s), (dn_g, up_s), (dn_g, dn_s)]
    partner = (g, s + 1 - 2 * c)

    near = corners + [z_peer(i) for i in Z_NEAR] + [xy_peer(i)[1] for i in XY_ROW + XY_COLUMN] + sides + [partner]

    def load(src, dst, n):
        copy = pltpu.make_async_copy(src, dst, ld.at[n])
        copy.start()
        return copy

    for device in near:
        greet(device)
    flow_loads = [load(vel, vel_v, 0), load(rate, rate_v, 2), load(forc, forc_v, 3)]
    mom_load = load(mom, mz.at[z], 1)
    other_loads = [load(spec, spec_v, 4), load(dense, dense_v, 5), load(tab, tab_v, 6), load(assign, asg_v, 7)]
    other_loads += [load(aline_h, aline, 8), load(az_h, az, 9)]

    def send(src, dst, n, device):
        return pltpu.make_async_remote_copy(
            src_ref=src, dst_ref=dst, send_sem=ssem.at[n], recv_sem=rsem.at[n], device_id=device, device_id_type=MESH
        )

    def arrived(buf, count, n):
        send(buf.at[pl.ds(0, count)], buf.at[pl.ds(0, count)], n, partner).wait_recv()

    def sent(buf, count, n):
        send(buf.at[pl.ds(0, count)], buf.at[pl.ds(0, count)], n, partner).wait_send()

    def tell(n, device):
        pl.semaphore_signal(know.at[n], inc=1, device_id=device, device_id_type=MESH)

    row = iota((8, 512), 0)

    def shifted(plane, before, after):
        lo = jnp.where(row == 0, before, pltpu.roll(plane, 1, axis=0))
        hi = jnp.where(row == 7, after, pltpu.roll(plane, 7, axis=0))
        return lo + hi

    def along(plane):
        return pltpu.roll(plane, 1, axis=1) + pltpu.roll(plane, 511, axis=1)

    for copy in flow_loads:
        copy.wait()
    for n, (a, b) in enumerate([(7, 6), (0, 1), (7, 6), (0, 1)]):
        pick = (lambda ref, i: ref[i]) if n < 2 else (lambda ref, i: ref[:, i, :])
        mid, far, r, f = pick(vel_v, a), pick(vel_v, b), pick(rate_v, a), pick(forc_v, a)
        side_snd[n, 0] = mid
        side_snd[n, 1] = mid + (r * (far + shifted(mid, 0.0, 0.0) + along(mid) - 6.0 * mid) + f)
        side_snd[n, 2] = r
    for n, (a, b) in enumerate([(7, 7), (7, 0), (0, 7), (0, 0)]):
        corn_snd[n] = vel_v[a, b : b + 1, :]
    pl.semaphore_wait(barrier, len(near))
    for n in range(4):
        send(side_snd.at[n], side_rcv.at[n], 0, sides[n]).start()
    for n in range(4):
        send(corn_snd.at[n], corn_rcv.at[n], 1, corners[n]).start()

    for i in (4, NZ - 4):
        tell(0, z_peer(i))
    for i in XY_COLUMN:
        tell(1, xy_peer(i)[1])

    for copy in other_loads:
        copy.wait()
    dv = dense_v[...]
    mixing = dv[:, 0:WIDTH]
    eye = iota((WIDTH, WIDTH), 0) == iota((WIDTH, WIDTH), 1)
    gain_row = jnp.sum(jnp.where(eye, dv[:, 64:65], 0.0), axis=0, keepdims=True)
    bias_row = jnp.sum(jnp.where(eye, dv[:, 65:66], 0.0), axis=0, keepdims=True)
    gain_lanes = jnp.concatenate([gain_row, gain_row], axis=1)
    bias_lanes = jnp.concatenate([bias_row, bias_row], axis=1)
    layer_bias = dv[:, 66:67]
    proj = dv[:, 67:68]
    m1 = jnp.sum(mixing * gain_row, axis=1, keepdims=True)
    m0 = jnp.sum(mixing * bias_row, axis=1, keepdims=True) + layer_bias
    weights = spec_v[...]
    segment = jnp.where(iota((32, 2048), 1) // WIDTH == iota((32, 2048), 0), 1.0, 0.0).astype(BF16)
    gain_high, gain_low = parts(weights * jnp.concatenate([gain_lanes] * 16, axis=1))
    bias_high, bias_low = parts(weights * jnp.concatenate([bias_lanes] * 16, axis=1))
    seen = nt(jnp.concatenate([gain_high, gain_low, bias_high, bias_low], axis=0), segment)
    lane16 = iota((WIDTH, 16), 1)
    left = jnp.concatenate(
        [
            seen[0:64] + seen[64:128],
            seen[128:192] + seen[192:256],
            jnp.where(lane16 == 0, m1, jnp.where(lane16 == 1, m0, 0.0)),
        ],
        axis=1,
    )
    left_high, left_low = parts(left)
    left3 = jnp.concatenate([left_high, left_high, left_low], axis=1)
    for row0, part in zip((32, 112, 192), [parts(tab_v[64:96, :])[i] for i in (0, 1, 0)]):
        for t in range(LINES):
            right[row0 : row0 + 32, SUB * t : SUB * (t + 1)] = part

    pl.semaphore_wait(know.at[1], 3)
    tell(2, partner)
    pl.semaphore_wait(know.at[0], 2)
    mom_load.wait()
    for i in Z_ORDER:
        send(mz.at[z], mz.at[z], 2, z_peer(i)).start()

    send(side_snd, side_rcv, 0, partner).wait_recv()
    has = [g > 0, g < NG - 1, s > 0, s < NS - 1]
    edge0 = [jnp.where(has[n], side_rcv[n, 0], 0.0) for n in range(4)]

    def flow(cells, edge):
        changes = []
        for x in range(8):
            mid = cells[x]
            below = edge[0] if x == 0 else cells[x - 1]
            above = edge[1] if x == 7 else cells[x + 1]
            beside = above + below + shifted(mid, edge[2][x : x + 1, :], edge[3][x : x + 1, :]) + along(mid)
            changes.append(rate_v[x] * (beside - 6.0 * mid) + forc_v[x])
        return changes

    first = [vel_v[x] for x in range(8)]
    second = [mid + change for mid, change in zip(first, flow(first, edge0))]
    for x in range(8):
        v1_s[8 * x : 8 * x + 8, :] = second[x]
    for t in range(LINES):
        samp[t : t + 1, :] = v1_s[pl.ds(aline[t], 1), :]
    row8 = iota((8, SUB), 0)

    def windows(tile):
        start = jnp.zeros((8, SUB), jnp.int32)
        for i in range(8):
            start = jnp.where(row8 == i, az[(tile % 2) * 8 + i], start)
        block, shift = start // SUB, start % SUB
        quarter = [samp[8 * tile : 8 * tile + 8, SUB * q : SUB * (q + 1)] for q in range(4)]
        lo = jnp.where(block == 0, quarter[0], jnp.where(block == 1, quarter[1], jnp.where(block == 2, quarter[2], quarter[3])))
        hi = jnp.where(block == 0, quarter[1], jnp.where(block == 1, quarter[2], quarter[3]))
        at = iota((8, SUB), 1) + shift
        index = at % SUB
        return jnp.where(at < SUB, take_lanes(lo, index), take_lanes(hi, index))

    inputs = jnp.concatenate([windows(0), windows(1)], axis=0)
    waves_of = nt(jnp.concatenate(parts(tab_v[0:32, :]), axis=0), jnp.concatenate(parts(inputs), axis=0))
    spectrum = waves_of[0:32, 0:LINES] + waves_of[0:32, LINES:] + waves_of[32:64, 0:LINES]
    cos_w, sin_w = tab_v[32:48, :], tab_v[48:64, :]
    row16 = iota((16, SUB), 0)
    for t in range(LINES):
        one = slice(SUB * t, SUB * (t + 1))
        ur, ui = spectrum[0:16, t : t + 1], spectrum[16:32, t : t + 1]
        waves = jnp.concatenate([ur * cos_w - ui * sin_w, -(ui * cos_w + ur * sin_w)], axis=0)
        high, low = parts(waves)
        right[0:32, one] = high
        right[80:112, one] = low
        right[160:192, one] = high
        rest = jnp.where(row16 == 0, inputs[t : t + 1, :], jnp.where(row16 == 1, 1.0, 0.0))
        high, low = parts(rest)
        right[64:80, one] = high
        right[144:160, one] = low
        right[224:240, one] = high

    send(corn_snd, corn_rcv, 1, partner).wait_recv()
    corner = [
        jnp.where(jnp.logical_and(has[a], has[b]), corn_rcv[n], 0.0)
        for n, (a, b) in enumerate([(0, 2), (0, 3), (1, 2), (1, 3)])
    ]
    edge1 = []
    for n, (a, lo, hi) in enumerate([(0, 0, 1), (7, 2, 3), (0, 0, 2), (7, 1, 3)]):
        part, r = [jnp.where(has[n], side_rcv[n, i], 0.0) for i in (1, 2)]
        own = vel_v[a] if n < 2 else vel_v[:, a, :]
        ends = jnp.where(row == 0, corner[lo], jnp.where(row == 7, corner[hi], 0.0))
        edge1.append(part + r * (own + ends))

    for x, change in enumerate(flow(second, edge1)):
        chg_s[8 * x : 8 * x + 8, :] = change
        field_o[x] = second[x] + change
    for t in range(LINES):
        samp[LINES + t : LINES + t + 1, :] = chg_s[pl.ds(aline[t], 1), :]
    targets = jnp.concatenate([windows(2), windows(3)], axis=0)

    scale = 1.0 / (TOTAL * SUB)
    proj_grad = jnp.zeros((WIDTH, SUB), F32)
    for pair in range(LINES // 2):
        cols = slice(2 * SUB * pair, 2 * SUB * (pair + 1))
        pre = nn(left3, right[:, cols])
        square = pre * pre
        bend = jnp.tanh(GELU_C * (pre + 0.044715 * (square * pre)))
        half_up = 0.5 * (1.0 + bend)
        hidden = pre * half_up
        slope = half_up + 0.5 * pre * (1.0 - bend * bend) * (GELU_C * (1.0 + 3.0 * 0.044715 * square))
        guess = jnp.sum(hidden * proj, axis=0, keepdims=True)
        target = jnp.concatenate([targets[2 * pair : 2 * pair + 1, :], targets[2 * pair + 1 : 2 * pair + 2, :]], axis=1)
        miss = guess - target
        diff_s[2 * pair : 2 * pair + 1, :] = miss[:, 0:SUB]
        diff_s[2 * pair + 1 : 2 * pair + 2, :] = miss[:, SUB:]
        dq = (2.0 * scale) * miss
        high, low = parts(slope * proj * dq)
        dp_s[0:64, cols] = high
        dp_s[64:128, cols] = low
        back = hidden * dq
        proj_grad = proj_grad + back[:, 0:SUB] + back[:, SUB:]
    grads = nt(dp_s[...], right[0:160, :])
    grads = grads[0:64, 0:KEEP] + grads[0:64, KEEP:] + grads[64:128, 0:KEEP]

    diff = diff_s[...]
    err = jnp.sum(diff * diff, axis=1, keepdims=True)
    eye16 = iota((LINES, LINES), 0) == iota((LINES, LINES), 1)
    err_row = jnp.sum(jnp.where(eye16, err, 0.0), axis=0, keepdims=True)
    named = iota((NS, LINES), 0) == asg_v[...]
    loss = jnp.sum(jnp.where(named, err_row, 0.0), axis=1, keepdims=True) / (LINES * SUB)

    keep = iota((WIDTH, KEEP), 1)
    grads = jnp.where(keep == LANE_PROJ, jnp.sum(proj_grad, axis=1, keepdims=True), grads)
    grads = jnp.where(keep == LANE_LOSS + g, loss, grads)
    payload = jnp.concatenate([grads, jnp.zeros((WIDTH, SUB - KEEP), F32)], axis=1)
    for p in range(8):
        pay[p] = payload[8 * p : 8 * p + 8, :]

    def scatter(order):
        for i in order:
            p, device = plane_peer(i)
            send(pay.at[p], rsb.at[me], 6, device).start()

    pl.semaphore_wait(know.at[2], 1)
    scatter(PLANE_ORDER)
    rsb[me] = pay[piece]
    arrived(rsb, 2 * NXY - 1, 6)
    zrb[z] = jnp.sum(rsb[...], axis=0)

    for i in Z_ORDER:
        send(zrb.at[z], zrb.at[z], 7, z_peer(i)).start()

    arrived(mz, NZ - 1, 2)
    turned = jnp.concatenate([mz[i] for i in range(NZ)], axis=0).T
    gath[c, xy] = jnp.concatenate([turned[0:32, :], turned[32:64, :]], axis=1)
    for i in XY_ORDER:
        send(gath.at[c, xy], gath.at[c, xy], 3, xy_peer(i)[1]).start()

    arrived(zrb, NZ - 1, 7)
    agb[piece] = jnp.sum(zrb[...], axis=0)
    for i in RING_ORDER:
        send(agb.at[piece], agb.at[piece], 4, plane_peer(i)[1]).start()

    arrived(gath.at[c], NXY - 1, 3)
    send(gath.at[c], gath.at[c], 5, partner).start()
    lane32 = iota((32, SUB), 1)

    def unpack(share, before):
        for j in range(16):
            for v in range(2):
                index = v * 64 + ((j % 2) * 8 + lane32 // 16) * 4 + lane32 % 4
                two = [take_lanes(gath[share, (j // 2) * 2 + h], index) for h in range(2)]
                moved = jnp.where((lane32 // 8) % 2 == 0, two[0], two[1])
                moved = jnp.where((lane32 // 4) % 2 == share, moved, 0.0)
                at = (slice(32 * v, 32 * v + 32), slice(SUB * j, SUB * (j + 1)))
                base_s[at] = before[at] - (learn_rate * decay_rate) * moved

    unpack(c, spec_v)
    send(gath.at[1 - c], gath.at[1 - c], 5, partner).wait_recv()
    unpack(1 - c, base_s)
    arrived(agb, 7, 4)
    total = agb[...].reshape(WIDTH, SUB)

    lane = iota((WIDTH, SUB), 1)
    gain_back = jnp.zeros((WIDTH, SUB), F32)
    bias_back = jnp.zeros((WIDTH, SUB), F32)
    for j in range(16):
        cols = slice(SUB * j, SUB * (j + 1))
        index = jnp.where(lane < 64, 2 * j, 2 * j + 1)
        by_gain = take_lanes(total, index + LANE_P)
        by_bias = take_lanes(total, index + LANE_Q)
        grad = gain_lanes * by_gain + bias_lanes * by_bias
        grad_s[:, cols] = grad
        spec_o[:, cols] = base_s[:, cols] - learn_rate * grad
        w = spec_v[:, cols]
        gain_back = gain_back + by_gain * w
        bias_back = bias_back + by_bias * w

    dm1, dm0 = total[:, LANE_M1 : LANE_M1 + 1], total[:, LANE_M0 : LANE_M0 + 1]

    def to_column(back, dm):
        both = jnp.sum(back, axis=0, keepdims=True)
        both = both[:, 0:WIDTH] + both[:, WIDTH:] + jnp.sum(mixing * dm, axis=0, keepdims=True)
        return jnp.sum(jnp.where(eye, both, 0.0), axis=1, keepdims=True)

    dense_o[:, 0:64] = mixing - dense_rate * (gain_row * dm1 + bias_row * dm0)
    dense_o[:, 64:65] = dv[:, 64:65] - dense_rate * to_column(gain_back, dm1)
    dense_o[:, 65:66] = dv[:, 65:66] - dense_rate * to_column(bias_back, dm0)
    dense_o[:, 66:67] = layer_bias - dense_rate * dm0
    dense_o[:, 67:68] = proj - dense_rate * total[:, LANE_PROJ : LANE_PROJ + 1]

    mine = grad_s[:, pl.ds(pl.multiple_of((d // 32) * SUB, SUB), SUB)]
    mine = pltpu.roll(mine, lax.rem(SUB - lax.rem(d, 32) * 4, SUB), axis=1)
    mom_o[...] = decay_rate * mz[z] + mine.T[0:4, :]

    own = jnp.logical_and(iota((NS, SUB), 0) == s, lane == LANE_LOSS + g)
    own = jnp.sum(jnp.where(own, total, 0.0), axis=1, keepdims=True)
    loss_o[...] = jnp.sum(own, axis=0, keepdims=True)

    send(side_snd, side_rcv, 0, partner).wait_send()
    send(corn_snd, corn_rcv, 1, partner).wait_send()
    sent(mz, NZ - 1, 2)
    sent(gath.at[c], NXY - 1, 3)
    send(gath.at[c], gath.at[c], 5, partner).wait_send()
    sent(rsb, 2 * NXY - 1, 6)
    sent(zrb, NZ - 1, 7)
    sent(agb, 7, 4)


def write(*refs):
    sources, results, sems = refs[:5], refs[5:10], refs[10]
    pairs = [(sources[2].at[pl.ds(16 * i, 16)], results[2].at[pl.ds(16 * i, 16)]) for i in range(4)]
    pairs += [(sources[0].at[pl.ds(4 * i, 4)], results[0].at[pl.ds(4 * i, 4)]) for i in range(2)]
    pairs += [(sources[i], results[i]) for i in (1, 3, 4)]
    copies = [pltpu.make_async_copy(a, b, sems.at[i]) for i, (a, b) in enumerate(pairs)]
    for copy in copies:
        copy.start()
    for copy in copies:
        copy.wait()


def local(velocity, rate, forcing, anchor_line, anchor_z, assign, spectral, dense, momentum):
    hbm = pl.BlockSpec(memory_space=pltpu.HBM)
    whole = pl.BlockSpec(memory_space=pltpu.VMEM)
    vmem = pltpu.VMEM
    shapes = (
        jax.ShapeDtypeStruct((8, 8, 512), F32),
        jax.ShapeDtypeStruct((1, 1), F32),
        jax.ShapeDtypeStruct((WIDTH, 2048), F32),
        jax.ShapeDtypeStruct((WIDTH, 68), F32),
        jax.ShapeDtypeStruct((4, WIDTH), F32),
    )

    def pin(x):
        return pltpu.with_memory_space_constraint(x, pltpu.HBM)

    velocity, rate, forcing, momentum = pin(velocity), pin(rate), pin(forcing), pin(momentum)
    anchor_line, anchor_z = pin(anchor_line), pin(anchor_z)
    results = pl.pallas_call(
        kernel,
        out_shape=shapes,
        in_specs=[hbm] * 10,
        out_specs=(whole,) * 5,
        scratch_shapes=[
            vmem((8, 8, 512), F32),
            vmem((8, 8, 512), F32),
            vmem((8, 8, 512), F32),
            vmem((1, LINES), jnp.int32),
            vmem((WIDTH, 2048), F32),
            vmem((WIDTH, 68), F32),
            vmem((96, SUB), F32),
            vmem((4, 3, 8, 512), F32),
            vmem((4, 3, 8, 512), F32),
            vmem((4, 1, 512), F32),
            vmem((4, 1, 512), F32),
            vmem((64, 512), F32),
            vmem((64, 512), F32),
            vmem((2 * LINES, 512), F32),
            vmem((LINES, SUB), F32),
            vmem((3 * KEEP, 2048), BF16),
            vmem((2 * WIDTH, 2048), BF16),
            vmem((NZ, 4, WIDTH), F32),
            vmem((2, NXY, 32, SUB), F32),
            vmem((WIDTH, 2048), F32),
            vmem((WIDTH, 2048), F32),
            vmem((8, 8, SUB), F32),
            vmem((2 * NXY, 8, SUB), F32),
            vmem((NZ, 8, SUB), F32),
            vmem((8, 8, SUB), F32),
            pltpu.SMEM((LINES,), jnp.int32),
            pltpu.SMEM((LINES,), jnp.int32),
            pltpu.SemaphoreType.DMA((10,)),
            pltpu.SemaphoreType.DMA((8,)),
            pltpu.SemaphoreType.DMA((8,)),
            pltpu.SemaphoreType.REGULAR((3,)),
        ],
        compiler_params=pltpu.CompilerParams(
            collective_id=0, has_side_effects=True, vmem_limit_bytes=32 * 1024 * 1024
        ),
    )(velocity, rate, forcing, anchor_line, anchor_z, pin(assign.T), pin(spectral.T), pin(dense.T), momentum, pin(jnp.asarray(tables())))
    field, loss, spec, dens, mom = pl.pallas_call(
        write,
        out_shape=shapes,
        in_specs=[pl.BlockSpec(memory_space=pl.ANY)] * 5,
        out_specs=(hbm,) * 5,
        scratch_shapes=[pltpu.SemaphoreType.DMA((9,))],
        compiler_params=pltpu.CompilerParams(vmem_limit_bytes=1024 * 1024),
    )(*results)
    return (field, loss, spec.T, dens.T, mom)


def solution(mesh):
    placed = (
        P("grp", "slab", None),
        P("grp", "slab", None),
        P("grp", "slab", None),
        P(("grp", "slab")),
        P(("grp", "slab")),
        P(("grp", "slab"), None),
        P(),
        P(),
        P(("grp", "slab"), None),
    )
    return jax.shard_map(
        local,
        mesh=mesh,
        in_specs=placed,
        out_specs=(P("grp", "slab", None), P("grp", "slab"), P(), P(), P(("grp", "slab"), None)),
        check_vma=False,
    )
```
